512 devices in a mesh: dp: 16 (over z, core), ctx: 32 (over y, x).
Axes of the slice: x: 4, y: 8, z: 8, core: 2. Of those that a mesh axis runs over, the one named last changes fastest.
Arguments:
- queries: bfloat16 [16, 4096, 2560], P('dp', 'ctx'), may hold values from -6 to 6
- keys: bfloat16 [16, 4096, 512], P('dp', 'ctx'), may hold values from -6 to 6
- values: bfloat16 [16, 4096, 512], P('dp', 'ctx'), may hold values from -6 to 6
- outputs: bfloat16 [16, 4096, 2560], P('dp', 'ctx'), may hold values from -6 to 6
- d_out: bfloat16 [16, 4096, 2560], P('dp', 'ctx'), may hold values from -6 to 6
- log_sums: float32 [16, 20, 4096], P('dp', None, 'ctx'), may hold values from 2 to 6
- block_path: int32 [16, 32], P('dp'), may hold values from 0 to 16, as said below
- live_len: int32 [16, 32], P('dp'), may hold values from 1 to 128, as said below
Outputs:
- grad_query: bfloat16 [16, 4096, 2560], P('dp', 'ctx')
- grad_key: bfloat16 [16, 4096, 512], P('dp', 'ctx')
- grad_value: bfloat16 [16, 4096, 512], P('dp', 'ctx')
- bias_grad: float32 [1024], P('dp')
The draws below stay inside these ranges and needn't reach their ends.
Inputs may be any that keep to these rules, and one draw needn't show every extreme that they name: `block_path`: for each sequence: one or two shared opening blocks and one or two shared closing blocks; the blocks between form 8 to 16 consecutive runs numbered 1, 2, ... in order, one run a path; some sequence has 16 paths. `live_len`: only the last block of a path may be partly live; every other block is full.
All inputs are finite; a program needn't handle non-finite values.
Results may differ from the reference program's by a relative error of at most 0.015.
Values may be sent and summed in bfloat16 or wider, within the bound.
A program may use at most 128 MiB of HBM per device.

```python
import jax
import jax.numpy as jnp
from jax import lax

QUERY_HEAD_COUNT = 20
KEY_VALUE_HEADS = 4
HEAD_WIDTH = 128
BLK = 128
SEQUENCE_COUNT = 16
SEQUENCE_TOKENS = 4096
NB = 32
PATHS_MAX = 16
PATHS_MIN = 8
N_CTX = 32


def path_layout(key):
    chosen = jax.random.randint(jax.random.fold_in(key, 101), (), 0, SEQUENCE_COUNT)
    slots = jnp.arange(NB, dtype=jnp.int32)

    def one_sequence(seq_key, seq_index):
        parts_keys = jax.random.split(seq_key, 4)
        opening = jax.random.randint(parts_keys[0], (), 1, 3)
        closing = jax.random.randint(parts_keys[1], (), 1, 3)
        middle = NB - opening - closing
        branches = jax.random.randint(parts_keys[2], (), PATHS_MIN, PATHS_MAX + 1)
        branches = jnp.where(seq_index == chosen, PATHS_MAX, branches)
        usable = (slots >= 1) & (slots < middle)
        scores = jax.random.randint(parts_keys[3], (NB,), 0, 1 << 20) * NB + slots
        scores = jnp.where(usable, scores, (1 << 30) + slots)
        order = jnp.argsort(scores, stable=True)
        ranks = jnp.zeros((NB,), jnp.int32).at[order].set(slots)
        starts = usable & (ranks < branches - 1)
        labels = 1 + jnp.cumsum(starts.astype(jnp.int32))
        offset = slots - opening
        inside = (offset >= 0) & (offset < middle)
        picked = jnp.take(labels, jnp.clip(offset, 0, NB - 1))
        return jnp.where(inside, picked, 0).astype(jnp.int32)
    seq_keys = jax.random.split(key, SEQUENCE_COUNT)
    return jax.vmap(one_sequence)(seq_keys, jnp.arange(SEQUENCE_COUNT, dtype=jnp.int32))


def draw_block_path(key, part):
    return path_layout(key)


def draw_live_len(key, part):
    layout = path_layout(key)
    key = jax.random.fold_in(key, 7)
    following = jnp.concatenate([layout[:, 1:], jnp.zeros((SEQUENCE_COUNT, 1), jnp.int32)], axis=1)
    ending = (layout > 0) & (following != layout)
    partial_fill = jax.random.randint(key, (SEQUENCE_COUNT, NB), 1, BLK + 1)
    return jnp.where(ending, partial_fill, BLK).astype(jnp.int32)


def steps_of(own_key, dims, cuts, smallest, top_value):
    def one(dim, shards_of):
        draws = jax.random.uniform(jax.random.fold_in(jax.random.fold_in(own_key, 6), dim), (shards_of,), jnp.float32, smallest / len(cuts), top_value / len(cuts))
        return jnp.repeat(jnp.exp(draws), dims[dim] // shards_of).reshape((-1,) + (1,) * (len(dims) - dim - 1))

    factor_of = one(*cuts[0])
    for cut in cuts[1:]:
        factor_of = factor_of * one(*cut)
    return factor_of


def normal_values(stream_key, shape, scale, bound, pieces=(), held_as=jnp.bfloat16):
    factor_of = steps_of(stream_key, shape, pieces, -0.22, 0.18) if pieces else 1.0
    values = jax.random.normal(stream_key, shape, jnp.float32) * scale * factor_of
    return jnp.minimum(jnp.maximum(values, -bound), bound).astype(held_as)


def setup_inputs(seed: int = 0) -> dict:
    key_list = jax.random.split(jax.random.key(seed), 9)
    queries = normal_values(key_list[0], (SEQUENCE_COUNT, SEQUENCE_TOKENS, QUERY_HEAD_COUNT * HEAD_WIDTH), 1.0, 6.0, ((0, 16), (1, 32)))
    keys = normal_values(key_list[1], (SEQUENCE_COUNT, SEQUENCE_TOKENS, KEY_VALUE_HEADS * HEAD_WIDTH), 1.0, 6.0, ((0, 16), (1, 32)))
    values = normal_values(key_list[2], (SEQUENCE_COUNT, SEQUENCE_TOKENS, KEY_VALUE_HEADS * HEAD_WIDTH), 1.0, 6.0, ((0, 16), (1, 32)))
    outputs = normal_values(key_list[3], (SEQUENCE_COUNT, SEQUENCE_TOKENS, QUERY_HEAD_COUNT * HEAD_WIDTH), 1.0, 6.0, ((0, 16), (1, 32)))
    d_out = normal_values(key_list[4], (SEQUENCE_COUNT, SEQUENCE_TOKENS, QUERY_HEAD_COUNT * HEAD_WIDTH), 1.0, 6.0, ((0, 16), (1, 32)))
    log_sums = jnp.clip(2.0 + 4.0 * jax.random.uniform(key_list[5], (SEQUENCE_COUNT, QUERY_HEAD_COUNT, SEQUENCE_TOKENS), jnp.float32) ** steps_of(key_list[5], (SEQUENCE_COUNT, QUERY_HEAD_COUNT, SEQUENCE_TOKENS), ((0, 16), (2, 32)), -0.2, 0.2), 2.0, 6.0)
    block_path = draw_block_path(jax.random.fold_in(key_list[8], 71), 0)
    live_len = draw_live_len(jax.random.fold_in(key_list[8], 71), 0)
    return {"queries": queries, "keys": keys, "values": values, "outputs": outputs, "d_out": d_out, "log_sums": log_sums, "block_path": block_path, "live_len": live_len}


def rounded(field):
    return lax.optimization_barrier(field.astype(jnp.bfloat16)).astype(jnp.float32)


def visible(query_pos, key_pos, block_paths, live_counts, block_size):
    slots = jnp.arange(block_paths.shape[0], dtype=jnp.int32)
    shared = lax.cummax(jnp.where(block_paths == 0, slots, -1), axis=0)
    query_block = query_pos // block_size
    key_block = key_pos // block_size
    query_hot = (query_block[:, None] == slots[None, :]).astype(jnp.int32)
    key_hot = (key_block[:, None] == slots[None, :]).astype(jnp.int32)
    query_path = jnp.sum(query_hot * block_paths[None, :], axis=1)
    query_last = jnp.sum(query_hot * shared[None, :], axis=1)
    key_path = jnp.sum(key_hot * block_paths[None, :], axis=1)
    key_live = jnp.sum(key_hot * live_counts[None, :], axis=1)
    causal = key_pos[None, :] <= query_pos[:, None]
    filled = (key_pos % block_size) < key_live
    joined = (key_path == 0)[None, :] | (key_path[None, :] == query_path[:, None]) | (query_last[:, None] > key_block[None, :])
    return causal & filled[None, :] & joined


def sequence_grads(packed):
    queries, keys, values, outputs, d_out, log_sums, block_path, live_len = packed
    sequence_length = keys.shape[0]
    share_rows = sequence_length // N_CTX
    group_width = QUERY_HEAD_COUNT // KEY_VALUE_HEADS
    score_scale = HEAD_WIDTH ** -0.5
    query_heads = queries.astype(jnp.float32).reshape(sequence_length, QUERY_HEAD_COUNT, HEAD_WIDTH)
    grad_heads = d_out.astype(jnp.float32).reshape(sequence_length, QUERY_HEAD_COUNT, HEAD_WIDTH)
    deltas = jnp.sum(grad_heads * outputs.astype(jnp.float32).reshape(sequence_length, QUERY_HEAD_COUNT, HEAD_WIDTH), axis=2)
    log_sum = jnp.transpose(log_sums)
    key_head_count = keys.astype(jnp.float32).reshape(sequence_length, KEY_VALUE_HEADS, HEAD_WIDTH)
    value_head_count = values.astype(jnp.float32).reshape(sequence_length, KEY_VALUE_HEADS, HEAD_WIDTH)
    key_pos = jnp.arange(sequence_length, dtype=jnp.int32)

    def share(totals, share_index):
        first_row = share_index * share_rows
        query_pos = first_row + jnp.arange(share_rows, dtype=jnp.int32)
        allowed = visible(query_pos, key_pos, block_path, live_len, BLK)
        query_rows = lax.dynamic_slice_in_dim(query_heads, first_row, share_rows, 0)
        grad_rows = lax.dynamic_slice_in_dim(grad_heads, first_row, share_rows, 0)
        log_rows = lax.dynamic_slice_in_dim(log_sum, first_row, share_rows, 0)
        delta_rows = lax.dynamic_slice_in_dim(deltas, first_row, share_rows, 0)
        query_parts = []
        key_parts = []
        value_parts = []
        for head_index in range(KEY_VALUE_HEADS):
            lower = head_index * group_width
            upper = lower + group_width
            query_tile = query_rows[:, lower:upper]
            grad_tile = grad_rows[:, lower:upper]
            key_tile = key_head_count[:, head_index]
            value_tile = value_head_count[:, head_index]
            scores = jnp.einsum("qgd,kd->qgk", query_tile, key_tile) * score_scale
            weights_full = jnp.where(allowed[:, None, :], jnp.exp(scores - log_rows[:, lower:upper, None]), 0.0)
            weights_low = rounded(weights_full)
            value_parts.append(jnp.einsum("qgk,qgd->kd", weights_low, grad_tile))
            grad_weights = jnp.einsum("qgd,kd->qgk", grad_tile, value_tile)
            grad_scores = rounded(weights_full * (grad_weights - delta_rows[:, lower:upper, None]) * score_scale)
            query_parts.append(jnp.einsum("qgk,kd->qgd", grad_scores, key_tile).reshape(share_rows, group_width * HEAD_WIDTH))
            key_parts.append(jnp.einsum("qgk,qgd->kd", grad_scores, query_tile))
        partial_value = jnp.stack([jnp.concatenate(key_parts, axis=1), jnp.concatenate(value_parts, axis=1)])
        return totals + rounded(partial_value), jnp.concatenate(query_parts, axis=1)

    initial_totals = jnp.zeros((2, sequence_length, KEY_VALUE_HEADS * HEAD_WIDTH), jnp.float32)
    totals, query_grads = lax.scan(share, initial_totals, jnp.arange(N_CTX, dtype=jnp.int32))
    bias = jnp.concatenate([jnp.sum(totals[0], axis=0), jnp.sum(totals[1], axis=0)])
    grad_query = query_grads.reshape(sequence_length, QUERY_HEAD_COUNT * HEAD_WIDTH).astype(jnp.bfloat16)
    return grad_query, totals[0].astype(jnp.bfloat16), totals[1].astype(jnp.bfloat16), bias


def reference(queries, keys, values, outputs, d_out, log_sums, block_path, live_len):
    grad_query, grad_key, grad_value, biases = lax.map(sequence_grads, (queries, keys, values, outputs, d_out, log_sums, block_path, live_len))
    return grad_query, grad_key, grad_value, jnp.sum(biases, axis=0)
```

```python
import functools

import jax
import jax.numpy as jnp
from jax import lax
from jax.experimental import pallas as pl
from jax.experimental.pallas import tpu as pltpu
from jax.sharding import PartitionSpec as P

KV = 4
GROUP = 5
D = 128
BLK = 128
ROWS = 8
COLS = 4
NB = ROWS * COLS
DP = 16
GW = GROUP * D
SCALE = D**-0.5
LOG2E = 1.4426950408889634
MESH = pl.DeviceIdType.MESH
ANY = pl.BlockSpec(memory_space=pl.ANY)
VMEM = pl.BlockSpec(memory_space=pltpu.VMEM)
SMEM = pl.BlockSpec(memory_space=pltpu.SMEM)
NT = (((1,), (1,)), ((), ()))
TN = (((0,), (0,)), ((), ()))


def dot(a, b, dims=(((1,), (0,)), ((), ()))):
    return lax.dot_general(a, b, dims, preferred_element_type=jnp.float32)


def place():
    c = lax.axis_index("ctx")
    return lax.axis_index("dp"), c // COLS, c % COLS


def cols(start, size):
    return pl.ds(pl.multiple_of(start, 128), size)


def greet(targets):
    barrier = pltpu.get_barrier_semaphore()
    for target in targets:
        pl.semaphore_signal(barrier, inc=1, device_id=target, device_id_type=MESH)
    pl.semaphore_wait(barrier, len(targets))


def send(src, dst, send_sem, recv_sem, target):
    copy = pltpu.make_async_remote_copy(
        src_ref=src,
        dst_ref=dst,
        send_sem=send_sem,
        recv_sem=recv_sem,
        device_id=target,
        device_id_type=MESH,
    )
    copy.start()
    return copy


def gather_kernel(
    q, do, o, k, v, lse,
    qh, doh, kall, vall, stat,
    do_v, o_v, lse_v, stat_v,
    own_sem, load_sem, kv_s, kv_r, q_s, q_r, st_s, st_r, up_s, up_r, dn_s, dn_r,
):
    dp, y, x = place()
    peers = [(x + j) % COLS for j in range(1, COLS)]
    above = (dp, ((y + 1) % ROWS) * COLS + x)
    below = (dp, ((y + ROWS - 1) % ROWS) * COLS + x)
    loads = [
        pltpu.make_async_copy(do, do_v, load_sem.at[0]),
        pltpu.make_async_copy(o, o_v, load_sem.at[1]),
        pltpu.make_async_copy(lse, lse_v, load_sem.at[2]),
    ]
    for c in loads:
        c.start()
    greet([(dp, y * COLS + p) for p in peers] + [above, below])
    kv = []
    for j, p in enumerate(peers):
        to = (dp, y * COLS + p)
        for n, (src, dst) in enumerate(((k, kall), (v, vall))):
            kv.append(
                send(src.at[:, cols(p * D, D)], dst.at[y, x], kv_s.at[j, n], kv_r.at[j, n], to)
            )
    own = [
        pltpu.make_async_copy(k.at[:, cols(x * D, D)], kall.at[y, x], own_sem.at[0]),
        pltpu.make_async_copy(v.at[:, cols(x * D, D)], vall.at[y, x], own_sem.at[1]),
        pltpu.make_async_copy(q.at[:, cols(x * GW, GW)], qh.at[x], own_sem.at[2]),
        pltpu.make_async_copy(do.at[:, cols(x * GW, GW)], doh.at[x], own_sem.at[3]),
    ]
    for c in own:
        c.start()
    big = []
    for j, p in enumerate(peers):
        to = (dp, y * COLS + p)
        for n, (src, dst) in enumerate(((q, qh), (do, doh))):
            big.append(
                send(src.at[:, cols(p * GW, GW)], dst.at[x], q_s.at[j, n], q_r.at[j, n], to)
            )
    own[0].wait()
    own[1].wait()
    for c in kv:
        c.wait_recv()

    def ring(step):
        out = []
        up_block = (y + ROWS - step) % ROWS
        dn_block = (y + step) % ROWS
        for n, full in ((0, kall), (1, vall)):
            if step < 3 or n == 0:
                out.append(send(full.at[up_block], full.at[up_block], up_s.at[step, n], up_r.at[step, n], above))
            if step < 3 or n == 1:
                out.append(send(full.at[dn_block], full.at[dn_block], dn_s.at[step, n], dn_r.at[step, n], below))
        return out

    flying = ring(0)
    for c in loads:
        c.wait()
    ones = jnp.ones((8, D), jnp.bfloat16)
    stat_v[...] = jnp.zeros_like(stat_v)
    for h in range(KV * GROUP):
        g, i = divmod(h, GROUP)
        prod = do_v[:, h * D : (h + 1) * D].astype(jnp.float32) * o_v[
            :, h * D : (h + 1) * D
        ].astype(jnp.float32)
        hi = prod.astype(jnp.bfloat16)
        rest = prod - hi.astype(jnp.float32)
        mid = rest.astype(jnp.bfloat16)
        total = dot(ones, hi, NT) + dot(ones, mid, NT)
        stat_v[g, 8 + i : 9 + i, :] = total[0:1]
        stat_v[g, i : i + 1, :] = lse_v[h : h + 1, :] * LOG2E
    stats = []
    for j, p in enumerate(peers):
        stats.append(
            send(stat_v.at[p], stat.at[x], st_s.at[j], st_r.at[j], (dp, y * COLS + p))
        )
    mine = pltpu.make_async_copy(stat_v.at[x], stat.at[x], own_sem.at[4])
    mine.start()
    for step in range(1, 4):
        for c in flying:
            c.wait_recv()
        for c in flying:
            c.wait_send()
        flying = ring(step)
    for c in flying:
        c.wait()
    for c in kv:
        c.wait_send()
    for c in big + stats:
        c.wait()
    own[2].wait()
    own[3].wait()
    mine.wait()


def gather(q, do, o, k, v, lse):
    bf = jnp.bfloat16
    sem = pltpu.SemaphoreType.DMA
    return pl.pallas_call(
        gather_kernel,
        out_shape=(
            jax.ShapeDtypeStruct((COLS, BLK, GW), bf),
            jax.ShapeDtypeStruct((COLS, BLK, GW), bf),
            jax.ShapeDtypeStruct((ROWS, COLS, BLK, D), bf),
            jax.ShapeDtypeStruct((ROWS, COLS, BLK, D), bf),
            jax.ShapeDtypeStruct((COLS, 16, BLK), jnp.float32),
        ),
        in_specs=[ANY] * 6,
        out_specs=[ANY] * 5,
        scratch_shapes=[
            pltpu.VMEM((BLK, KV * GW), bf),
            pltpu.VMEM((BLK, KV * GW), bf),
            pltpu.VMEM((KV * GROUP, BLK), jnp.float32),
            pltpu.VMEM((COLS, 16, BLK), jnp.float32),
            sem((5,)), sem((3,)), sem((3, 2)), sem((3, 2)), sem((3, 2)), sem((3, 2)),
            sem((3,)), sem((3,)), sem((4, 2)), sem((4, 2)), sem((4, 2)), sem((4, 2)),
        ],
        compiler_params=pltpu.CompilerParams(
            collective_id=0, has_side_effects=True, vmem_limit_bytes=16 << 20
        ),
        name="gather",
    )(q, do, o, k, v, lse)


def attend_kernel(path, live, qh, doh, kall, vall, stat, dqh, part, bias, dk, dv, dqt):
    c = lax.axis_index("ctx")
    y = c // COLS
    rows = 256
    dk[...] = jnp.zeros_like(dk)
    dv[...] = jnp.zeros_like(dv)
    nopen = jnp.where(path[0, 1] == 0, 2, 1)
    key_row = lax.broadcasted_iota(jnp.int32, (rows, GW), 0)

    def pieces(i, kc, vc, keep):
        qi, gi = qh[i], doh[i]
        heads = lambda a: jnp.concatenate([a[:, n * D : (n + 1) * D] for n in range(GROUP)], axis=0)
        qs, gs = heads(qi), heads(gi)
        flat = lambda first: jnp.concatenate(
            [stat[i, first + n : first + n + 1, :] for n in range(GROUP)], axis=1
        )
        s = dot(kc, qs, NT)
        p = jnp.where(keep, jnp.exp2(s * (SCALE * LOG2E) - flat(0)), 0.0)
        t = dot(vc, gs, NT)
        ds = (p * (t - flat(8))).astype(jnp.bfloat16)
        return dot(ds, qs), dot(p.astype(jnp.bfloat16), gs), dot(kc, ds, TN)

    for i in range(COLS):
        b = y * COLS + i
        mine = path[0, b]
        at = pl.ds(pl.multiple_of(b * BLK, BLK), BLK)
        query_col = lax.broadcasted_iota(jnp.int32, (BLK, GW), 1) % BLK
        row = lax.broadcasted_iota(jnp.int32, (BLK, GW), 0)
        keep = (row <= query_col) & (row < live[0, b])
        a, v_part, q_part = pieces(i, kall[at, :], vall[at, :], keep)
        dk[at, :] += a
        dv[at, :] += v_part
        dqt[...] = q_part
        start = lax.while_loop(
            lambda r: (r > 0) & (path[0, jnp.maximum(r - 1, 0)] == mine), lambda r: r - 1, b
        )
        shared = mine == 0
        first_end = jnp.where(shared, 0, nopen)
        start = jnp.where(shared, 0, start)

        def span(lower, upper):
            def step(n, _):
                kb = lower + 2 * n
                two = pl.ds(pl.multiple_of(kb * BLK, BLK), rows)
                second = jnp.where(kb + 1 < upper, live[0, jnp.minimum(kb + 1, NB - 1)], 0)
                keep = key_row < jnp.where(key_row < BLK, live[0, kb], BLK + second)
                a, v_part, q_part = pieces(i, kall[two, :], vall[two, :], keep)
                dk[two, :] += a
                dv[two, :] += v_part
                dqt[...] += q_part
                return 0

            lax.fori_loop(0, (upper - lower + 1) // 2, step, 0)

        span(0, first_end)
        span(start, b)
        for n in range(GROUP):
            dqh[i, :, n * D : (n + 1) * D] = (
                dqt[:, n * D : (n + 1) * D] * SCALE
            ).T.astype(jnp.bfloat16)

    bias[...] = jnp.zeros_like(bias)

    def finish(n, sums):
        at = pl.ds(pl.multiple_of(n * 512, 512), 512)
        a = dk[at, :] * SCALE
        b = dv[at, :]
        part[n, 0] = a.astype(jnp.bfloat16)
        part[n, 1] = b.astype(jnp.bfloat16)
        return (
            sums[0] + jnp.sum(a, axis=0, keepdims=True),
            sums[1] + jnp.sum(b, axis=0, keepdims=True),
        )

    zero = jnp.zeros((1, D), jnp.float32)
    ka, va = lax.fori_loop(0, ROWS, finish, (zero, zero))
    bias[0:1, :] = ka
    bias[1:2, :] = va


def attend(path, live, qh, doh, kall, vall, stat):
    bf = jnp.bfloat16
    return pl.pallas_call(
        attend_kernel,
        out_shape=(
            jax.ShapeDtypeStruct((COLS, BLK, GW), bf),
            jax.ShapeDtypeStruct((ROWS, 2, COLS * BLK, D), bf),
            jax.ShapeDtypeStruct((8, D), jnp.float32),
        ),
        in_specs=[SMEM, SMEM] + [VMEM] * 5,
        out_specs=[VMEM] * 3,
        scratch_shapes=[
            pltpu.VMEM((NB * BLK, D), jnp.float32),
            pltpu.VMEM((NB * BLK, D), jnp.float32),
            pltpu.VMEM((BLK, GW), jnp.float32),
        ],
        compiler_params=pltpu.CompilerParams(vmem_limit_bytes=40 << 20),
        name="attend",
    )(path, live, qh, doh, kall.reshape(NB * BLK, D), vall.reshape(NB * BLK, D), stat)


def give_back_kernel(
    dqh, part, biasp,
    dq, dkv_k, dkv_v, bias,
    down, up, down_out, up_out, final, by, bd, bx,
    own_sem, q_s, q_r, dn_s, dn_r, up_s, up_r, f_s, f_r, y_s, y_r, d_s, d_r, x_s, x_r,
):
    dp, y, x = place()
    c = y * COLS + x
    peers = [(x + j) % COLS for j in range(1, COLS)]
    above = (dp, ((y + 1) % ROWS) * COLS + x)
    below = (dp, ((y + ROWS - 1) % ROWS) * COLS + x)
    in_row = [(dp, y * COLS + p) for p in peers]
    in_col = [(dp, ((y + j) % ROWS) * COLS + x) for j in range(1, ROWS)]
    in_dp = [((dp + j) % DP, c) for j in range(1, DP)]
    greet(in_row + in_col + in_dp)

    def ring(step):
        out = []
        owner_dn = (y + ROWS - 4 + step) % ROWS
        owner_up = (y + 4 - step) % ROWS
        for n in (0, 1):
            for way, owner, land, stage, ss, rs, to, first in (
                (0, owner_dn, down, down_out, dn_s, dn_r, below, n),
                (1, owner_up, up, up_out, up_s, up_r, above, 1 - n),
            ):
                if step < first:
                    continue
                if step == first:
                    src = part.at[owner, n]
                else:
                    before[way, n].wait_recv()
                    stage[step, n] = (
                        land[step - 1, n].astype(jnp.float32)
                        + part[owner, n].astype(jnp.float32)
                    ).astype(jnp.bfloat16)
                    src = stage.at[step, n]
                copy = send(src, land.at[step, n], ss.at[step, n], rs.at[step, n], to)
                before[way, n] = copy
                out.append(copy)
        return out

    before = {}
    started = ring(0)
    by[y] = biasp[...]
    col = [send(by.at[y], by.at[y], y_s.at[j], y_r.at[j], t) for j, t in enumerate(in_col)]
    own_q = pltpu.make_async_copy(dqh.at[x], dq.at[:, cols(x * GW, GW)], own_sem.at[0])
    own_q.start()
    back = [
        send(dqh.at[p], dq.at[:, cols(x * GW, GW)], q_s.at[j], q_r.at[j], in_row[j])
        for j, p in enumerate(peers)
    ]
    started += ring(1)
    for copy in col:
        copy.wait()
    bd[dp] = jnp.sum(by[...], axis=0)
    deep = [send(bd.at[dp], bd.at[dp], d_s.at[j], d_r.at[j], t) for j, t in enumerate(in_dp)]
    started += ring(2)
    for copy in deep:
        copy.wait()
    bx[x] = jnp.sum(bd[...], axis=0)
    wide = [send(bx.at[x], bx.at[x], x_s.at[j], x_r.at[j], t) for j, t in enumerate(in_row)]
    started += ring(3)
    for copy in wide:
        copy.wait()
    entry = bx[(dp % 8) // 2]
    picked = jnp.where(dp < 8, entry[0:1], entry[1:2])
    swapped = jnp.concatenate([picked[:, 64:], picked[:, :64]], axis=1)
    bias[...] = jnp.where(dp % 2 == 0, picked, swapped)
    last = []
    for n, dst in ((0, dkv_k), (1, dkv_v)):
        before[0, n].wait_recv()
        before[1, n].wait_recv()
        total = (
            part[y, n].astype(jnp.float32)
            + down[3, n].astype(jnp.float32)
            + up[3, n].astype(jnp.float32)
        )
        final[n] = total.astype(jnp.bfloat16).reshape(COLS, BLK, D)
        for j, p in enumerate(peers):
            last.append(
                send(final.at[n, p], dst.at[:, cols(x * D, D)], f_s.at[j, n], f_r.at[j, n], in_row[j])
            )
        last_own = pltpu.make_async_copy(
            final.at[n, x], dst.at[:, cols(x * D, D)], own_sem.at[1 + n]
        )
        last_own.start()
        last.append(last_own)
    for copy in started:
        copy.wait_send()
    for copy in back:
        copy.wait()
    own_q.wait()
    for copy in last:
        copy.wait()


def give_back(dqh, part, biasp):
    bf = jnp.bfloat16
    sem = pltpu.SemaphoreType.DMA
    land = pltpu.VMEM((4, 2, COLS * BLK, D), bf)
    return pl.pallas_call(
        give_back_kernel,
        out_shape=(
            jax.ShapeDtypeStruct((BLK, KV * GW), bf),
            jax.ShapeDtypeStruct((BLK, KV * D), bf),
            jax.ShapeDtypeStruct((BLK, KV * D), bf),
            jax.ShapeDtypeStruct((1, D), jnp.float32),
        ),
        in_specs=[ANY, VMEM, VMEM],
        out_specs=[ANY, ANY, ANY, VMEM],
        scratch_shapes=[
            land, land, land, land,
            pltpu.VMEM((2, COLS, BLK, D), bf),
            pltpu.VMEM((ROWS, 8, D), jnp.float32),
            pltpu.VMEM((DP, 8, D), jnp.float32),
            pltpu.VMEM((COLS, 8, D), jnp.float32),
            sem((3,)), sem((3,)), sem((3,)),
            sem((4, 2)), sem((4, 2)), sem((4, 2)), sem((4, 2)),
            sem((3, 2)), sem((3, 2)),
            sem((7,)), sem((7,)), sem((15,)), sem((15,)), sem((3,)), sem((3,)),
        ],
        compiler_params=pltpu.CompilerParams(
            collective_id=1, has_side_effects=True, vmem_limit_bytes=32 << 20
        ),
        name="give_back",
    )(dqh, part, biasp)


def on_device(queries, keys, values, outputs, d_out, log_sums, block_path, live_len):
    qh, doh, kall, vall, stat = gather(
        queries[0], d_out[0], outputs[0], keys[0], values[0], log_sums[0]
    )
    dqh, part, biasp = attend(block_path, live_len, qh, doh, kall, vall, stat)
    dq, dk, dv, bias = give_back(dqh, part, biasp)
    return dq[None], dk[None], dv[None], bias[0, :64]


def solution(mesh):
    wide = P("dp", "ctx", None)
    return jax.shard_map(
        on_device,
        mesh=mesh,
        in_specs=(wide, wide, wide, wide, wide, P("dp", None, "ctx"), P("dp", None), P("dp", None)),
        out_specs=(wide, wide, wide, P("dp")),
        check_vma=False,
    )
```

```python
import functools

import jax
import jax.numpy as jnp
from jax import lax
from jax.experimental import pallas as pl
from jax.experimental.pallas import tpu as pltpu
from jax.sharding import PartitionSpec as P

KV = 4
GROUP = 5
D = 128
BLK = 128
ROWS = 8
COLS = 4
NB = ROWS * COLS
DP = 16
GW = GROUP * D
SCALE = D**-0.5
LOG2E = 1.4426950408889634
FAR = 1e30
FAR_ROWS = ROWS - 3
LIMIT = 60 << 20
MESH = pl.DeviceIdType.MESH
ANY = pl.BlockSpec(memory_space=pl.ANY)
VMEM = pl.BlockSpec(memory_space=pltpu.VMEM)
SMEM = pl.BlockSpec(memory_space=pltpu.SMEM)
NT = (((1,), (1,)), ((), ()))
TN = (((0,), (0,)), ((), ()))


def dot(a, b, dims=(((1,), (0,)), ((), ()))):
    return lax.dot_general(a, b, dims, preferred_element_type=jnp.float32)


def place():
    c = lax.axis_index("ctx")
    return lax.axis_index("dp"), c // COLS, c % COLS


def cols(start, size):
    return pl.ds(pl.multiple_of(start, 128), size)


def greet(targets):
    barrier = pltpu.get_barrier_semaphore()
    for target in targets:
        pl.semaphore_signal(barrier, inc=1, device_id=target, device_id_type=MESH)
    pl.semaphore_wait(barrier, len(targets))


def send(src, dst, send_sem, recv_sem, target):
    copy = pltpu.make_async_remote_copy(
        src_ref=src,
        dst_ref=dst,
        send_sem=send_sem,
        recv_sem=recv_sem,
        device_id=target,
        device_id_type=MESH,
    )
    copy.start()
    return copy


def unit(i, b, row, x, path, kc, vc, qref, gref, stat, dk_at, dv_at, dqt):
    heads = lambda a: jnp.concatenate([a[:, n * D : (n + 1) * D] for n in range(GROUP)], axis=0)
    flat = lambda first: jnp.concatenate(
        [stat[i, first + n : first + n + 1, :] for n in range(GROUP)], axis=1
    )
    qs, gs = heads(qref[i]), heads(gref[i])
    base, delta = flat(0), flat(8)
    mine = path[0, b]
    s = dot(kc, qs, NT)
    t = dot(vc, gs, NT)
    behind = lax.broadcasted_iota(jnp.int32, (BLK, GW), 0) - (
        lax.broadcasted_iota(jnp.int32, (BLK, GW), 1) % BLK
    )
    p_low, ds = [], []
    for j in range(COLS):
        kb = row * COLS + (x + j) % COLS
        theirs = path[0, kb]
        joined = (theirs == 0) | (theirs == mine) | (mine == 0)
        shift = base + jnp.where(joined, 0.0, FAR)
        at = slice(j * BLK, (j + 1) * BLK)
        p = jnp.exp2(s[at] * (SCALE * LOG2E) - shift)
        p = jnp.where(behind <= BLK * (b - kb), p, 0.0)
        p_low.append(p.astype(jnp.bfloat16))
        ds.append((p * (t[at] - delta)).astype(jnp.bfloat16))
    p_low = jnp.concatenate(p_low, axis=0)
    ds = jnp.concatenate(ds, axis=0)
    dk_at[...] += dot(ds, qs)
    dv_at[...] += dot(p_low, gs)
    dqt[i] += dot(kc, ds, TN)


def close_row(row, x, live, dk_at, dv_at, part_at, sums):
    key_row = lax.broadcasted_iota(jnp.int32, (BLK, D), 0)
    ka, va = sums
    for j in range(COLS):
        at = slice(j * BLK, (j + 1) * BLK)
        keep = key_row < live[0, row * COLS + (x + j) % COLS]
        a = jnp.where(keep, dk_at[at, :] * SCALE, 0.0)
        b = jnp.where(keep, dv_at[at, :], 0.0)
        part_at[0, at, :] = a.astype(jnp.bfloat16)
        part_at[1, at, :] = b.astype(jnp.bfloat16)
        ka += jnp.sum(a, axis=0, keepdims=True)
        va += jnp.sum(b, axis=0, keepdims=True)
    return ka, va


def no_sums():
    return jnp.zeros((1, D), jnp.float32), jnp.zeros((1, D), jnp.float32)


def gather_kernel(
    path, live, q, do, o, k, v, lse,
    qh, doh, stat, dqt_out, near_out, far, bias,
    do_v, o_v, lse_v, k_v, own_stat, q_v, g_v, kv_all, stat_v, dk, dv, dqt, near_v,
    own_sem, load_sem, out_sem, kv_s, kv_r, q_s, q_r, st_s, st_r, up_s, up_r, dn_s, dn_r,
):
    dp, y, x = place()
    c = y * COLS + x
    peers = [(x + j) % COLS for j in range(1, COLS)]
    above = (dp, ((y + 1) % ROWS) * COLS + x)
    below = (dp, ((y + ROWS - 1) % ROWS) * COLS + x)
    spot = lambda j: pl.ds(j * BLK, BLK)
    rest = pl.ds(BLK, 3 * BLK)
    loads = [
        pltpu.make_async_copy(k, k_v, load_sem.at[0]),
        pltpu.make_async_copy(do, do_v, load_sem.at[1]),
        pltpu.make_async_copy(o, o_v, load_sem.at[2]),
        pltpu.make_async_copy(lse, lse_v, load_sem.at[3]),
    ]
    for copy in loads:
        copy.start()
    own_q = [
        pltpu.make_async_copy(q.at[:, cols(x * GW, GW)], q_v.at[x], own_sem.at[2]),
        pltpu.make_async_copy(do.at[:, cols(x * GW, GW)], g_v.at[x], own_sem.at[3]),
    ]
    own_v = pltpu.make_async_copy(v.at[:, cols(x * D, D)], kv_all.at[y, 1, spot(0)], own_sem.at[1])
    for copy in own_q + [own_v]:
        copy.start()
    greet([(dp, y * COLS + p) for p in peers] + [above, below])
    kv, big = {}, {}
    for j, p in enumerate(peers):
        kv[j, 1] = send(
            v.at[:, cols(p * D, D)], kv_all.at[y, 1, spot(3 - j)], kv_s.at[j, 1], kv_r.at[j, 1],
            (dp, y * COLS + p),
        )
    loads[0].wait()
    key_row = lax.broadcasted_iota(jnp.int32, (BLK, KV * D), 0)
    k_v[...] = jnp.where(key_row < live[0, c], k_v[...].astype(jnp.float32), 0.0).astype(
        jnp.bfloat16
    )
    for j, p in enumerate(peers):
        kv[j, 0] = send(
            k_v.at[:, cols(p * D, D)], kv_all.at[y, 0, spot(3 - j)], kv_s.at[j, 0], kv_r.at[j, 0],
            (dp, y * COLS + p),
        )
    own_k = pltpu.make_async_copy(k_v.at[:, cols(x * D, D)], kv_all.at[y, 0, spot(0)], own_sem.at[0])
    own_k.start()
    ring = {}

    def piece(block, n, part):
        full = kv_all.at[block]
        if part == 0:
            return full.at[:, spot(0)] if n is None else full.at[n, spot(0)]
        return full.at[part - 1, rest]

    def forward(step, part):
        up_block = (y + ROWS - step) % ROWS
        dn_block = (y + step) % ROWS
        half = None if step < 3 else 0
        if step:
            ring[step - 1, part, 0].wait_recv()
        if step < 3 or part != 2:
            at = piece(up_block, half, part)
            ring[step, part, 0] = send(
                at, at, up_s.at[step, part], up_r.at[step, part], above
            )
        if step:
            ring[step - 1, part, 1].wait_recv()
        if step < 3 or part != 1:
            at = piece(dn_block, None if step < 3 else 1, part)
            ring[step, part, 1] = send(
                at, at, dn_s.at[step, part], dn_r.at[step, part], below
            )

    own_v.wait()
    own_k.wait()
    forward(0, 0)
    for j in range(3):
        kv[j, 1].wait_recv()
    forward(0, 2)
    for j in range(3):
        kv[j, 0].wait_recv()
    forward(0, 1)

    def move(*which):
        for j in which:
            for n, (src, dst) in enumerate(((q, q_v), (do, g_v))):
                big[j, n] = send(
                    src.at[:, cols(peers[j] * GW, GW)], dst.at[x], q_s.at[j, n], q_r.at[j, n],
                    (dp, y * COLS + peers[j]),
                )

    move(0, 2)
    for copy in loads[1:]:
        copy.wait()
    ones = jnp.ones((8, D), jnp.bfloat16)
    own_stat[...] = jnp.zeros_like(own_stat)
    for h in range(KV * GROUP):
        g, i = divmod(h, GROUP)
        prod = do_v[:, h * D : (h + 1) * D].astype(jnp.float32) * o_v[
            :, h * D : (h + 1) * D
        ].astype(jnp.float32)
        hi = prod.astype(jnp.bfloat16)
        mid = (prod - hi.astype(jnp.float32)).astype(jnp.bfloat16)
        total = dot(ones, hi, NT) + dot(ones, mid, NT)
        own_stat[g, 8 + i : 9 + i, :] = total[0:1]
        own_stat[g, i : i + 1, :] = lse_v[h] * LOG2E
    stats = [
        send(own_stat.at[p], stat_v.at[x], st_s.at[j], st_r.at[j], (dp, y * COLS + p))
        for j, p in enumerate(peers)
    ]
    mine = pltpu.make_async_copy(own_stat.at[x], stat_v.at[x], own_sem.at[4])
    mine.start()
    dk[...] = jnp.zeros_like(dk)
    dv[...] = jnp.zeros_like(dv)
    dqt[...] = jnp.zeros_like(dqt)

    def pairs(i, row, slot, valid):
        @pl.when(valid)
        def _():
            unit(
                i % COLS, y * COLS + i % COLS, row, x, path, kv_all[row, 0], kv_all[row, 1],
                q_v, g_v, stat_v, dk.at[slot], dv.at[slot], dqt,
            )

    def own_pair(j):
        pairs(x + j, y, 0, y >= 0)

    def last_pair(j):
        pairs(x + j, jnp.maximum(y - 1, 0), 1, y >= 1)

    def back_pair(j):
        pairs(x + j, jnp.maximum(y - 2, 0), 2, y >= 2)

    def open_pair(j):
        pairs(x + j, 0, 3, y >= 6)

    mine.wait()
    for copy in own_q:
        copy.wait()
    forward(1, 0)
    own_pair(0)
    forward(1, 2)
    forward(1, 1)
    move(1)
    last_pair(0)
    for j in (0, 2):
        stats[j].wait_recv()
        big[j, 0].wait_recv()
        big[j, 1].wait_recv()
    forward(2, 0)
    own_pair(1)
    forward(2, 2)
    own_pair(3)
    forward(2, 1)
    last_pair(1)
    last_pair(3)
    back_pair(0)
    forward(3, 0)
    back_pair(1)
    back_pair(3)
    open_pair(0)
    forward(3, 2)
    open_pair(1)
    open_pair(3)
    forward(3, 1)
    stats[1].wait_recv()
    big[1, 0].wait_recv()
    big[1, 1].wait_recv()
    outs = [
        pltpu.make_async_copy(q_v, qh, out_sem.at[0]),
        pltpu.make_async_copy(g_v, doh, out_sem.at[1]),
        pltpu.make_async_copy(stat_v, stat, out_sem.at[2]),
    ]
    for copy in outs:
        copy.start()
    own_pair(2)
    last_pair(2)
    back_pair(2)
    open_pair(2)
    outs.append(pltpu.make_async_copy(dqt, dqt_out, out_sem.at[5]))
    outs[-1].start()
    sums = no_sums()
    for slot, row in enumerate((y, (y + ROWS - 1) % ROWS, (y + ROWS - 2) % ROWS, 0)):
        sums = close_row(row, x, live, dk.at[slot], dv.at[slot], near_v.at[slot], sums)
    outs.append(pltpu.make_async_copy(near_v, near_out, out_sem.at[6]))
    outs[-1].start()
    bias[...] = jnp.zeros_like(bias)
    bias[0:1, :] = sums[0]
    bias[1:2, :] = sums[1]
    for part, way in ((0, 0), (1, 0), (0, 1), (2, 1)):
        ring[3, part, way].wait_recv()
    ends = [pltpu.make_async_copy(kv_all.at[pl.ds(0, FAR_ROWS)], far, out_sem.at[8])]
    for copy in ends:
        copy.start()
    for copy in list(ring.values()) + list(kv.values()) + list(big.values()) + stats:
        copy.wait_send()
    for copy in outs + ends:
        copy.wait()


def gather(path, live, q, do, o, k, v, lse):
    bf = jnp.bfloat16
    f32 = jnp.float32
    sem = pltpu.SemaphoreType.DMA
    rows = COLS * BLK
    heads = ((COLS, BLK, GW), bf)
    whole = ((ROWS, 2, rows, D), bf)
    far = ((FAR_ROWS, 2, rows, D), bf)
    stat = ((COLS, 16, BLK), f32)
    dqt = ((COLS, BLK, GW), f32)
    near = ((4, 2, rows, D), bf)
    outs = [heads, heads, stat, dqt, near, far, ((8, D), f32)]
    full = ((BLK, KV * GW), bf)
    slots = ((4, rows, D), f32)
    scratch = [
        full, full, ((KV * GROUP, 1, BLK), f32), ((BLK, KV * D), bf), stat,
        heads, heads, whole, stat, slots, slots, dqt, near,
    ]
    return pl.pallas_call(
        gather_kernel,
        out_shape=tuple(jax.ShapeDtypeStruct(*s) for s in outs),
        in_specs=[SMEM, SMEM] + [ANY] * 6,
        out_specs=[ANY] * 6 + [VMEM],
        scratch_shapes=[pltpu.VMEM(*s) for s in scratch] + [
            sem((5,)), sem((4,)), sem((9,)), sem((3, 2)), sem((3, 2)), sem((3, 2)), sem((3, 2)),
            sem((3,)), sem((3,)), sem((4, 3)), sem((4, 3)), sem((4, 3)), sem((4, 3)),
        ],
        compiler_params=pltpu.CompilerParams(
            collective_id=0, has_side_effects=True, vmem_limit_bytes=LIMIT
        ),
        name="gather",
    )(path, live, q, do, o, k, v, lse)


def attend_kernel(
    path, live, qh, doh, stat, dqt_near, far, near, bias_near,
    part, dqh, bias,
    q_v, g_v, stat_v, far_v, part_v, dk, dv, dqt, dqh_v, sem, near_sem, out_sem,
):
    y = lax.axis_index("ctx") // COLS
    x = lax.axis_index("ctx") % COLS
    early = y >= 6
    lower = jnp.where(early, 1, 0)
    upper = jnp.maximum(y - 2, 0)
    some = upper > lower
    placed = (
        (0, y, y >= 0), (1, y - 1, y >= 1), (2, y - 2, y >= 2), (3, 0, early),
    )
    near_copy = lambda slot, row: pltpu.make_async_copy(
        near.at[slot], part_v.at[row], near_sem.at[slot]
    )
    loads = [
        pltpu.make_async_copy(src, dst, sem.at[n])
        for n, (src, dst) in enumerate(
            ((far, far_v), (qh, q_v), (stat, stat_v), (doh, g_v))
        )
    ]

    @pl.when(some)
    def _():
        for copy in loads:
            copy.start()

    for slot, row, valid in placed:

        @pl.when(valid)
        def _(slot=slot, row=row):
            near_copy(slot, row).start()

    def blank(n, _):
        part_v[n] = jnp.zeros((2, COLS * BLK, D), jnp.bfloat16)
        return 0

    lax.fori_loop(y + 1, ROWS, blank, 0)
    out_q = pltpu.make_async_copy(dqh_v, dqh, out_sem.at[0])
    load_q = pltpu.make_async_copy(dqt_near, dqt, sem.at[4])
    load_q.start()

    def clear(n, _):
        dk[n] = jnp.zeros((COLS * BLK, D), jnp.float32)
        dv[n] = jnp.zeros((COLS * BLK, D), jnp.float32)
        return 0

    lax.fori_loop(lower, upper, clear, 0)
    load_q.wait()

    @pl.when(some)
    def _():
        for copy in loads:
            copy.wait()

        def query(i, _):
            b = y * COLS + i
            mine = path[0, b]

            def one(row, _):
                seen = lambda kb: (path[0, kb] == 0) | (path[0, kb] == mine) | (mine == 0)
                kb = row * COLS
                needed = seen(kb) | seen(kb + 1) | seen(kb + 2) | seen(kb + 3)

                @pl.when(needed)
                def _():
                    unit(
                        i, b, row, x, path, far_v[row, 0], far_v[row, 1], q_v, g_v, stat_v,
                        dk.at[row], dv.at[row], dqt,
                    )

                return 0

            lax.fori_loop(lower, upper, one, 0)
            return 0

        lax.fori_loop(0, COLS, query, 0)

    def finish_query(i, _):
        for n in range(GROUP):
            at = slice(n * D, (n + 1) * D)
            dqh_v[i, :, at] = (dqt[i, :, at] * SCALE).T.astype(jnp.bfloat16)
        return 0

    lax.fori_loop(0, COLS, finish_query, 0)
    out_q.start()

    sums = lax.fori_loop(
        lower,
        upper,
        lambda n, s: close_row(n, x, live, dk.at[n], dv.at[n], part_v.at[n], s),
        (bias_near[0:1, :], bias_near[1:2, :]),
    )
    bias[...] = jnp.zeros_like(bias)
    bias[0:1, :] = sums[0]
    bias[1:2, :] = sums[1]
    for slot, row, valid in placed:

        @pl.when(valid)
        def _(slot=slot, row=row):
            near_copy(slot, row).wait()

    out_part = pltpu.make_async_copy(part_v, part, out_sem.at[1])
    out_part.start()
    out_part.wait()
    out_q.wait()


def attend(path, live, qh, doh, stat, dqt_near, far, near, bias_near):
    bf = jnp.bfloat16
    f32 = jnp.float32
    rows = COLS * BLK
    sem = pltpu.SemaphoreType.DMA
    heads = ((COLS, BLK, GW), bf)
    kept = ((FAR_ROWS, 2, rows, D), bf)
    part = ((ROWS, 2, rows, D), bf)
    dqt = ((COLS, BLK, GW), f32)
    grads = ((FAR_ROWS, rows, D), f32)
    scratch = [heads, heads, ((COLS, 16, BLK), f32), kept, part, grads, grads, dqt, heads]
    return pl.pallas_call(
        attend_kernel,
        out_shape=tuple(jax.ShapeDtypeStruct(*s) for s in (part, heads, ((8, D), f32))),
        in_specs=[SMEM, SMEM] + [ANY] * 6 + [VMEM],
        out_specs=[ANY, ANY, VMEM],
        scratch_shapes=[pltpu.VMEM(*s) for s in scratch] + [sem((5,)), sem((4,)), sem((2,))],
        compiler_params=pltpu.CompilerParams(vmem_limit_bytes=LIMIT),
        name="attend",
    )(path, live, qh, doh, stat, dqt_near, far, near, bias_near)


def flip(value, bit):
    return value + bit - 2 * bit * ((value // bit) % 2)


def give_back_kernel(
    part, biasp, dqh,
    dq, dkv_k, dkv_v, bias,
    part_v, down, up, down_out, up_out, final, totals, inbox, bx, bd,
    load_sem, own_sem, q_s, q_r, dn_s, dn_r, up_s, up_r, f_s, f_r, b_s, b_r, x_s, x_r, d_s, d_r,
):
    dp, y, x = place()
    c = y * COLS + x
    peers = [(x + j) % COLS for j in range(1, COLS)]
    above = (dp, ((y + 1) % ROWS) * COLS + x)
    below = (dp, ((y + ROWS - 1) % ROWS) * COLS + x)
    in_row = [(dp, y * COLS + p) for p in peers]
    fold = [(dp, flip(y, bit) * COLS + x) for bit in (1, 2, 4)]
    deep = [(dp + j) % DP for j in range(1, DP)]
    load = pltpu.make_async_copy(part, part_v, load_sem.at[0])
    load.start()
    greet(in_row + [above, below] + fold[1:] + [(to, c) for to in deep])
    before = {}
    started = []

    def hop(step, n, way):
        first = n if way == 0 else 1 - n
        land, stage, ss, rs, to = (
            (down, down_out, dn_s, dn_r, below), (up, up_out, up_s, up_r, above),
        )[way]
        owner = (y + ROWS - 4 + step) % ROWS if way == 0 else (y + 4 - step) % ROWS
        if step == first:
            src = part.at[owner, n]
        else:
            before[way, n].wait_recv()
            stage[step, n] = (
                land[step - 1, n].astype(jnp.float32) + part_v[owner, n].astype(jnp.float32)
            ).astype(jnp.bfloat16)
            src = stage.at[step, n]
        before[way, n] = send(src, land.at[step, n], ss.at[step, n], rs.at[step, n], to)
        started.append(before[way, n])

    hop(0, 0, 0)
    hop(0, 1, 1)
    hop(1, 1, 0)
    hop(1, 0, 1)
    own_q = pltpu.make_async_copy(dqh.at[x], dq.at[:, cols(x * GW, GW)], own_sem.at[0])
    own_q.start()
    back = [
        send(dqh.at[p], dq.at[:, cols(x * GW, GW)], q_s.at[j], q_r.at[j], in_row[j])
        for j, p in enumerate(peers)
    ]
    totals[0] = biasp[...]
    folds = []

    def fold_next():
        n = len(folds)
        if n:
            folds[-1].wait_recv()
            totals[n] = totals[n - 1] + inbox[n - 1]
        if n < len(fold):
            folds.append(send(totals.at[n], inbox.at[n], b_s.at[n], b_r.at[n], fold[n]))

    fold_next()
    load.wait()
    hop(1, 0, 0)
    hop(1, 1, 1)
    fold_next()
    hop(2, 1, 0)
    hop(2, 0, 1)
    fold_next()
    hop(2, 0, 0)
    hop(2, 1, 1)
    fold_next()
    bx[x] = totals[len(fold)]
    wide = [send(bx.at[x], bx.at[x], x_s.at[j], x_r.at[j], t) for j, t in enumerate(in_row)]
    hop(3, 1, 0)
    hop(3, 0, 1)
    for copy in wide:
        copy.wait()
    across = [
        send(bx.at[(to % 8) // 2], bd.at[dp], d_s.at[j], d_r.at[j], (to, c))
        for j, to in enumerate(deep)
    ]
    bd[dp] = bx[(dp % 8) // 2]
    hop(3, 0, 0)
    hop(3, 1, 1)
    last = []
    for n, dst in ((1, dkv_v), (0, dkv_k)):
        before[0, n].wait_recv()
        before[1, n].wait_recv()
        total = (
            part_v[y, n].astype(jnp.float32)
            + down[3, n].astype(jnp.float32)
            + up[3, n].astype(jnp.float32)
        )
        final[n] = total.astype(jnp.bfloat16).reshape(COLS, BLK, D)
        for j, p in enumerate(peers):
            last.append(
                send(final.at[n, j + 1], dst.at[:, cols(x * D, D)], f_s.at[j, n], f_r.at[j, n], in_row[j])
            )
        last_own = pltpu.make_async_copy(
            final.at[n, 0], dst.at[:, cols(x * D, D)], own_sem.at[1 + n]
        )
        last_own.start()
        last.append(last_own)
    for copy in started + folds:
        copy.wait_send()
    for copy in back:
        copy.wait()
    own_q.wait()
    for copy in last + across:
        copy.wait()
    entry = jnp.sum(bd[...], axis=0)
    picked = jnp.where(dp < 8, entry[0:1], entry[1:2])
    swapped = jnp.concatenate([picked[:, 64:], picked[:, :64]], axis=1)
    bias[...] = jnp.where(dp % 2 == 0, picked, swapped)


def give_back(part, biasp, dqh):
    bf = jnp.bfloat16
    f32 = jnp.float32
    sem = pltpu.SemaphoreType.DMA
    rows = COLS * BLK
    land = ((4, 2, rows, D), bf)
    scratch = [
        ((ROWS, 2, rows, D), bf), land, land, land, land, ((2, COLS, BLK, D), bf),
        ((4, 8, D), f32), ((3, 8, D), f32), ((COLS, 8, D), f32), ((DP, 8, D), f32),
    ]
    outs = (((BLK, KV * GW), bf), ((BLK, KV * D), bf), ((BLK, KV * D), bf), ((1, D), f32))
    return pl.pallas_call(
        give_back_kernel,
        out_shape=tuple(jax.ShapeDtypeStruct(*s) for s in outs),
        in_specs=[ANY, VMEM, ANY],
        out_specs=[ANY, ANY, ANY, VMEM],
        scratch_shapes=[pltpu.VMEM(*s) for s in scratch] + [
            sem((1,)), sem((3,)), sem((3,)), sem((3,)),
            sem((4, 2)), sem((4, 2)), sem((4, 2)), sem((4, 2)),
            sem((3, 2)), sem((3, 2)),
            sem((3,)), sem((3,)), sem((3,)), sem((3,)), sem((15,)), sem((15,)),
        ],
        compiler_params=pltpu.CompilerParams(
            collective_id=1, has_side_effects=True, vmem_limit_bytes=LIMIT
        ),
        name="give_back",
    )(part, biasp, dqh)


def store_kernel(dq, dk, dv, bias, dq_out, dk_out, dv_out, bias_out, dq_v, dk_v, dv_v, sem):
    moves = []
    for n in range(4):
        rows = pl.ds(n * 32, 32)
        moves.append((dq.at[rows], dq_v.at[rows], dq_out.at[rows]))
    moves.append((dk, dk_v, dk_out))
    moves.append((dv, dv_v, dv_out))
    first = [pltpu.make_async_copy(m[0], m[1], sem.at[0, n]) for n, m in enumerate(moves)]
    second = [pltpu.make_async_copy(m[1], m[2], sem.at[1, n]) for n, m in enumerate(moves)]
    for copy in first:
        copy.start()
    bias_out[...] = bias[0, :64]
    for one, two in zip(first, second):
        one.wait()
        two.start()
    for copy in second:
        copy.wait()


def store(dq, dk, dv, bias):
    shape = lambda a: jax.ShapeDtypeStruct(a.shape, a.dtype)
    return pl.pallas_call(
        store_kernel,
        out_shape=(shape(dq), shape(dk), shape(dv), jax.ShapeDtypeStruct((64,), jnp.float32)),
        in_specs=[ANY, ANY, ANY, VMEM],
        out_specs=[ANY, ANY, ANY, VMEM],
        scratch_shapes=[pltpu.VMEM(a.shape, a.dtype) for a in (dq, dk, dv)]
        + [pltpu.SemaphoreType.DMA((2, 6))],
        compiler_params=pltpu.CompilerParams(vmem_limit_bytes=LIMIT),
        name="store",
    )(dq, dk, dv, bias)


def on_device(queries, keys, values, outputs, d_out, log_sums, block_path, live_len):
    gathered = gather(
        block_path, live_len,
        queries[0], d_out[0], outputs[0], keys[0], values[0], jnp.transpose(log_sums, (1, 0, 2)),
    )
    qh, doh, stat, dqt_near, near, far, bias_near = gathered
    part, dqh, biasp = attend(
        block_path, live_len, qh, doh, stat, dqt_near, far, near, bias_near
    )
    dq, dk, dv, bias = store(*give_back(part, biasp, dqh))
    return dq[None], dk[None], dv[None], bias


def solution(mesh):
    wide = P("dp", "ctx", None)
    return jax.shard_map(
        on_device,
        mesh=mesh,
        in_specs=(wide, wide, wide, wide, wide, P("dp", None, "ctx"), P("dp", None), P("dp", None)),
        out_specs=(wide, wide, wide, P("dp")),
        check_vma=False,
    )
```

```python
import functools

import jax
import jax.numpy as jnp
from jax import lax
from jax.experimental import pallas as pl
from jax.experimental.pallas import tpu as pltpu
from jax.sharding import PartitionSpec as P

KV = 4
GROUP = 5
D = 128
BLK = 128
ROWS = 8
COLS = 4
NB = ROWS * COLS
DP = 16
GW = GROUP * D
SCALE = D**-0.5
LOG2E = 1.4426950408889634
FAR = 1e30
FAR_ROWS = ROWS - 3
LIMIT = 60 << 20
MESH = pl.DeviceIdType.MESH
ANY = pl.BlockSpec(memory_space=pl.ANY)
VMEM = pl.BlockSpec(memory_space=pltpu.VMEM)
SMEM = pl.BlockSpec(memory_space=pltpu.SMEM)
NT = (((1,), (1,)), ((), ()))
TN = (((0,), (0,)), ((), ()))


def dot(a, b, dims=(((1,), (0,)), ((), ()))):
    return lax.dot_general(a, b, dims, preferred_element_type=jnp.float32)


def place():
    c = lax.axis_index("ctx")
    return lax.axis_index("dp"), c // COLS, c % COLS


def cols(start, size):
    return pl.ds(pl.multiple_of(start, 128), size)


def greet(targets):
    barrier = pltpu.get_barrier_semaphore()
    for target in targets:
        pl.semaphore_signal(barrier, inc=1, device_id=target, device_id_type=MESH)
    pl.semaphore_wait(barrier, len(targets))


def send(src, dst, send_sem, recv_sem, target):
    copy = pltpu.make_async_remote_copy(
        src_ref=src,
        dst_ref=dst,
        send_sem=send_sem,
        recv_sem=recv_sem,
        device_id=target,
        device_id_type=MESH,
    )
    copy.start()
    return copy


def unit(i, b, row, x, path, kc, vc, qref, gref, stat, dk_at, dv_at, dqt):
    heads = lambda a: jnp.concatenate([a[:, n * D : (n + 1) * D] for n in range(GROUP)], axis=0)
    flat = lambda first: jnp.concatenate(
        [stat[i, first + n : first + n + 1, :] for n in range(GROUP)], axis=1
    )
    qs, gs = heads(qref[i]), heads(gref[i])
    base, delta = flat(0), flat(8)
    mine = path[0, b]
    s = dot(kc, qs, NT)
    t = dot(vc, gs, NT)
    behind = lax.broadcasted_iota(jnp.int32, (BLK, GW), 0) - (
        lax.broadcasted_iota(jnp.int32, (BLK, GW), 1) % BLK
    )
    p_low, ds = [], []
    for j in range(COLS):
        kb = row * COLS + (x + j) % COLS
        theirs = path[0, kb]
        joined = (theirs == 0) | (theirs == mine) | (mine == 0)
        shift = base + jnp.where(joined, 0.0, FAR)
        at = slice(j * BLK, (j + 1) * BLK)
        p = jnp.exp2(s[at] * (SCALE * LOG2E) - shift)
        p = jnp.where(behind <= BLK * (b - kb), p, 0.0)
        p_low.append(p.astype(jnp.bfloat16))
        ds.append((p * (t[at] - delta)).astype(jnp.bfloat16))
    p_low = jnp.concatenate(p_low, axis=0)
    ds = jnp.concatenate(ds, axis=0)
    dk_at[...] += dot(ds, qs)
    dv_at[...] += dot(p_low, gs)
    dqt[i] += dot(kc, ds, TN)


def close_row(row, x, live, dk_at, dv_at, part_at, sums):
    key_row = lax.broadcasted_iota(jnp.int32, (BLK, D), 0)
    ka, va = sums
    for j in range(COLS):
        at = slice(j * BLK, (j + 1) * BLK)
        keep = key_row < live[0, row * COLS + (x + j) % COLS]
        a = jnp.where(keep, dk_at[at, :] * SCALE, 0.0)
        b = jnp.where(keep, dv_at[at, :], 0.0)
        part_at[0, at, :] = a.astype(jnp.bfloat16)
        part_at[1, at, :] = b.astype(jnp.bfloat16)
        ka += jnp.sum(a, axis=0, keepdims=True)
        va += jnp.sum(b, axis=0, keepdims=True)
    return ka, va


def no_sums():
    return jnp.zeros((1, D), jnp.float32), jnp.zeros((1, D), jnp.float32)


def gather_kernel(
    path, live, q, do, o, k, v, lse,
    qh, doh, stat, dqt_out, near_out, far, bias,
    do_v, o_v, lse_v, k_v, own_stat, q_v, g_v, kv_all, stat_v, dk, dv, dqt, near_v,
    own_sem, load_sem, out_sem, kv_s, kv_r, q_s, q_r, st_s, st_r, up_s, up_r, dn_s, dn_r,
):
    dp, y, x = place()
    c = y * COLS + x
    peers = [(x + j) % COLS for j in range(1, COLS)]
    above = (dp, ((y + 1) % ROWS) * COLS + x)
    below = (dp, ((y + ROWS - 1) % ROWS) * COLS + x)
    spot = lambda j: pl.ds(j * BLK, BLK)
    rest = pl.ds(BLK, 3 * BLK)
    loads = [
        pltpu.make_async_copy(k, k_v, load_sem.at[0]),
        pltpu.make_async_copy(do, do_v, load_sem.at[1]),
        pltpu.make_async_copy(o, o_v, load_sem.at[2]),
        pltpu.make_async_copy(lse, lse_v, load_sem.at[3]),
    ]
    for copy in loads:
        copy.start()
    own_q = [
        pltpu.make_async_copy(q.at[:, cols(x * GW, GW)], q_v.at[x], own_sem.at[2]),
        pltpu.make_async_copy(do.at[:, cols(x * GW, GW)], g_v.at[x], own_sem.at[3]),
    ]
    own_v = pltpu.make_async_copy(v.at[:, cols(x * D, D)], kv_all.at[y, 1, spot(0)], own_sem.at[1])
    for copy in own_q + [own_v]:
        copy.start()
    greet([(dp, y * COLS + p) for p in peers] + [above, below])
    kv, big = {}, {}
    for j, p in enumerate(peers):
        kv[j, 1] = send(
            v.at[:, cols(p * D, D)], kv_all.at[y, 1, spot(3 - j)], kv_s.at[j, 1], kv_r.at[j, 1],
            (dp, y * COLS + p),
        )
    loads[0].wait()
    key_row = lax.broadcasted_iota(jnp.int32, (BLK, KV * D), 0)
    k_v[...] = jnp.where(key_row < live[0, c], k_v[...].astype(jnp.float32), 0.0).astype(
        jnp.bfloat16
    )
    for j, p in enumerate(peers):
        kv[j, 0] = send(
            k_v.at[:, cols(p * D, D)], kv_all.at[y, 0, spot(3 - j)], kv_s.at[j, 0], kv_r.at[j, 0],
            (dp, y * COLS + p),
        )
    own_k = pltpu.make_async_copy(k_v.at[:, cols(x * D, D)], kv_all.at[y, 0, spot(0)], own_sem.at[0])
    own_k.start()
    ring = {}

    def piece(block, n, part):
        full = kv_all.at[block]
        if part == 0:
            return full.at[:, spot(0)] if n is None else full.at[n, spot(0)]
        return full.at[part - 1, rest]

    def forward(step, part):
        up_block = (y + ROWS - step) % ROWS
        dn_block = (y + step) % ROWS
        half = None if step < 3 else 0
        if step:
            ring[step - 1, part, 0].wait_recv()
        if step < 3 or part != 2:
            at = piece(up_block, half, part)
            ring[step, part, 0] = send(
                at, at, up_s.at[step, part], up_r.at[step, part], above
            )
        if step:
            ring[step - 1, part, 1].wait_recv()
        if step < 3 or part != 1:
            at = piece(dn_block, None if step < 3 else 1, part)
            ring[step, part, 1] = send(
                at, at, dn_s.at[step, part], dn_r.at[step, part], below
            )

    own_v.wait()
    own_k.wait()
    forward(0, 0)
    for j in range(3):
        kv[j, 1].wait_recv()
    forward(0, 2)
    for j in range(3):
        kv[j, 0].wait_recv()
    forward(0, 1)

    def move(*which):
        for j in which:
            for n, (src, dst) in enumerate(((q, q_v), (do, g_v))):
                big[j, n] = send(
                    src.at[:, cols(peers[j] * GW, GW)], dst.at[x], q_s.at[j, n], q_r.at[j, n],
                    (dp, y * COLS + peers[j]),
                )

    move(0, 2)
    for copy in loads[1:]:
        copy.wait()
    ones = jnp.ones((8, D), jnp.bfloat16)
    own_stat[...] = jnp.zeros_like(own_stat)
    for h in range(KV * GROUP):
        g, i = divmod(h, GROUP)
        prod = do_v[:, h * D : (h + 1) * D].astype(jnp.float32) * o_v[
            :, h * D : (h + 1) * D
        ].astype(jnp.float32)
        hi = prod.astype(jnp.bfloat16)
        mid = (prod - hi.astype(jnp.float32)).astype(jnp.bfloat16)
        total = dot(ones, hi, NT) + dot(ones, mid, NT)
        own_stat[g, 8 + i : 9 + i, :] = total[0:1]
        own_stat[g, i : i + 1, :] = lse_v[h] * LOG2E
    stats = [
        send(own_stat.at[p], stat_v.at[x], st_s.at[j], st_r.at[j], (dp, y * COLS + p))
        for j, p in enumerate(peers)
    ]
    mine = pltpu.make_async_copy(own_stat.at[x], stat_v.at[x], own_sem.at[4])
    mine.start()
    dk[...] = jnp.zeros_like(dk)
    dv[...] = jnp.zeros_like(dv)
    dqt[...] = jnp.zeros_like(dqt)

    def pairs(i, row, slot, valid):
        @pl.when(valid)
        def _():
            unit(
                i % COLS, y * COLS + i % COLS, row, x, path, kv_all[row, 0], kv_all[row, 1],
                q_v, g_v, stat_v, dk.at[slot], dv.at[slot], dqt,
            )

    def own_pair(j):
        pairs(x + j, y, 0, y >= 0)

    def last_pair(j):
        pairs(x + j, jnp.maximum(y - 1, 0), 1, y >= 1)

    def back_pair(j):
        pairs(x + j, jnp.maximum(y - 2, 0), 2, y >= 2)

    def open_pair(j):
        pairs(x + j, 0, 3, y >= 6)

    mine.wait()
    for copy in own_q:
        copy.wait()
    forward(1, 0)
    move(1)
    own_pair(0)
    forward(1, 2)
    forward(1, 1)
    last_pair(0)
    for j in (0, 2):
        stats[j].wait_recv()
        big[j, 0].wait_recv()
        big[j, 1].wait_recv()
    forward(2, 0)
    own_pair(1)
    forward(2, 2)
    own_pair(3)
    forward(2, 1)
    last_pair(1)
    last_pair(3)
    back_pair(0)
    forward(3, 0)
    back_pair(1)
    back_pair(3)
    open_pair(0)
    forward(3, 2)
    open_pair(1)
    open_pair(3)
    forward(3, 1)
    stats[1].wait_recv()
    big[1, 0].wait_recv()
    big[1, 1].wait_recv()
    outs = [
        pltpu.make_async_copy(q_v, qh, out_sem.at[0]),
        pltpu.make_async_copy(g_v, doh, out_sem.at[1]),
        pltpu.make_async_copy(stat_v, stat, out_sem.at[2]),
    ]
    for copy in outs:
        copy.start()
    own_pair(2)
    last_pair(2)
    back_pair(2)
    open_pair(2)
    outs.append(pltpu.make_async_copy(dqt, dqt_out, out_sem.at[5]))
    outs[-1].start()
    sums = no_sums()
    for slot, row in enumerate((y, (y + ROWS - 1) % ROWS, (y + ROWS - 2) % ROWS, 0)):
        sums = close_row(row, x, live, dk.at[slot], dv.at[slot], near_v.at[slot], sums)
    outs.append(pltpu.make_async_copy(near_v, near_out, out_sem.at[6]))
    outs[-1].start()
    bias[...] = jnp.zeros_like(bias)
    bias[0:1, :] = sums[0]
    bias[1:2, :] = sums[1]
    for part, way in ((0, 0), (1, 0), (0, 1), (2, 1)):
        ring[3, part, way].wait_recv()
    ends = [pltpu.make_async_copy(kv_all.at[pl.ds(0, FAR_ROWS)], far, out_sem.at[8])]
    for copy in ends:
        copy.start()
    for copy in list(ring.values()) + list(kv.values()) + list(big.values()) + stats:
        copy.wait_send()
    for copy in outs + ends:
        copy.wait()


def gather(path, live, q, do, o, k, v, lse):
    bf = jnp.bfloat16
    f32 = jnp.float32
    sem = pltpu.SemaphoreType.DMA
    rows = COLS * BLK
    heads = ((COLS, BLK, GW), bf)
    whole = ((ROWS, 2, rows, D), bf)
    far = ((FAR_ROWS, 2, rows, D), bf)
    stat = ((COLS, 16, BLK), f32)
    dqt = ((COLS, BLK, GW), f32)
    near = ((4, 2, rows, D), bf)
    outs = [heads, heads, stat, dqt, near, far, ((8, D), f32)]
    full = ((BLK, KV * GW), bf)
    slots = ((4, rows, D), f32)
    scratch = [
        full, full, ((KV * GROUP, 1, BLK), f32), ((BLK, KV * D), bf), stat,
        heads, heads, whole, stat, slots, slots, dqt, near,
    ]
    return pl.pallas_call(
        gather_kernel,
        out_shape=tuple(jax.ShapeDtypeStruct(*s) for s in outs),
        in_specs=[SMEM, SMEM] + [ANY] * 6,
        out_specs=[ANY] * 6 + [VMEM],
        scratch_shapes=[pltpu.VMEM(*s) for s in scratch] + [
            sem((5,)), sem((4,)), sem((9,)), sem((3, 2)), sem((3, 2)), sem((3, 2)), sem((3, 2)),
            sem((3,)), sem((3,)), sem((4, 3)), sem((4, 3)), sem((4, 3)), sem((4, 3)),
        ],
        compiler_params=pltpu.CompilerParams(
            collective_id=0, has_side_effects=True, vmem_limit_bytes=LIMIT
        ),
        name="gather",
    )(path, live, q, do, o, k, v, lse)


def attend_kernel(
    path, live, qh, doh, stat, dqt_near, far, near, bias_near,
    part, dqh, bias,
    q_v, g_v, stat_v, far_v, part_v, dk, dv, dqt, dqh_v, sem, near_sem, out_sem,
):
    y = lax.axis_index("ctx") // COLS
    x = lax.axis_index("ctx") % COLS
    early = y >= 6
    lower = jnp.where(early, 1, 0)
    upper = jnp.maximum(y - 2, 0)
    some = upper > lower
    placed = (
        (0, y, y >= 0), (1, y - 1, y >= 1), (2, y - 2, y >= 2), (3, 0, early),
    )
    near_copy = lambda slot, row: pltpu.make_async_copy(
        near.at[slot], part_v.at[row], near_sem.at[slot]
    )
    loads = [
        pltpu.make_async_copy(src, dst, sem.at[n])
        for n, (src, dst) in enumerate(
            ((far, far_v), (qh, q_v), (stat, stat_v), (doh, g_v))
        )
    ]

    @pl.when(some)
    def _():
        for copy in loads:
            copy.start()

    for slot, row, valid in placed:

        @pl.when(valid)
        def _(slot=slot, row=row):
            near_copy(slot, row).start()

    def blank(n, _):
        part_v[n] = jnp.zeros((2, COLS * BLK, D), jnp.bfloat16)
        return 0

    lax.fori_loop(y + 1, ROWS, blank, 0)
    out_q = pltpu.make_async_copy(dqh_v, dqh, out_sem.at[0])
    load_q = pltpu.make_async_copy(dqt_near, dqt, sem.at[4])
    load_q.start()

    def clear(n, _):
        dk[n] = jnp.zeros((COLS * BLK, D), jnp.float32)
        dv[n] = jnp.zeros((COLS * BLK, D), jnp.float32)
        return 0

    lax.fori_loop(lower, upper, clear, 0)
    load_q.wait()

    @pl.when(some)
    def _():
        for copy in loads:
            copy.wait()

        def query(i, _):
            b = y * COLS + i
            mine = path[0, b]

            def one(row, _):
                seen = lambda kb: (path[0, kb] == 0) | (path[0, kb] == mine) | (mine == 0)
                kb = row * COLS
                needed = seen(kb) | seen(kb + 1) | seen(kb + 2) | seen(kb + 3)

                @pl.when(needed)
                def _():
                    unit(
                        i, b, row, x, path, far_v[row, 0], far_v[row, 1], q_v, g_v, stat_v,
                        dk.at[row], dv.at[row], dqt,
                    )

                return 0

            lax.fori_loop(lower, upper, one, 0)
            return 0

        lax.fori_loop(0, COLS, query, 0)

    def finish_query(i, _):
        for n in range(GROUP):
            at = slice(n * D, (n + 1) * D)
            dqh_v[i, :, at] = (dqt[i, :, at] * SCALE).T.astype(jnp.bfloat16)
        return 0

    lax.fori_loop(0, COLS, finish_query, 0)
    out_q.start()

    sums = lax.fori_loop(
        lower,
        upper,
        lambda n, s: close_row(n, x, live, dk.at[n], dv.at[n], part_v.at[n], s),
        (bias_near[0:1, :], bias_near[1:2, :]),
    )
    bias[...] = jnp.zeros_like(bias)
    bias[0:1, :] = sums[0]
    bias[1:2, :] = sums[1]
    for slot, row, valid in placed:

        @pl.when(valid)
        def _(slot=slot, row=row):
            near_copy(slot, row).wait()

    out_part = pltpu.make_async_copy(part_v, part, out_sem.at[1])
    out_part.start()
    out_part.wait()
    out_q.wait()


def attend(path, live, qh, doh, stat, dqt_near, far, near, bias_near):
    bf = jnp.bfloat16
    f32 = jnp.float32
    rows = COLS * BLK
    sem = pltpu.SemaphoreType.DMA
    heads = ((COLS, BLK, GW), bf)
    kept = ((FAR_ROWS, 2, rows, D), bf)
    part = ((ROWS, 2, rows, D), bf)
    dqt = ((COLS, BLK, GW), f32)
    grads = ((FAR_ROWS, rows, D), f32)
    scratch = [heads, heads, ((COLS, 16, BLK), f32), kept, part, grads, grads, dqt, heads]
    return pl.pallas_call(
        attend_kernel,
        out_shape=tuple(jax.ShapeDtypeStruct(*s) for s in (part, heads, ((8, D), f32))),
        in_specs=[SMEM, SMEM] + [ANY] * 6 + [VMEM],
        out_specs=[ANY, ANY, VMEM],
        scratch_shapes=[pltpu.VMEM(*s) for s in scratch] + [sem((5,)), sem((4,)), sem((2,))],
        compiler_params=pltpu.CompilerParams(vmem_limit_bytes=LIMIT),
        name="attend",
    )(path, live, qh, doh, stat, dqt_near, far, near, bias_near)


def give_back_kernel(
    part, biasp, dqh,
    dq, dkv_k, dkv_v, bias,
    part_v, down, up, down_out, up_out, final, by, bx, twin, bz,
    load_sem, own_sem, q_s, q_r, dn_s, dn_r, up_s, up_r, f_s, f_r, y_s, y_r, x_s, x_r, t_s, t_r, d_s, d_r,
):
    dp, y, x = place()
    c = y * COLS + x
    peers = [(x + j) % COLS for j in range(1, COLS)]
    above = (dp, ((y + 1) % ROWS) * COLS + x)
    below = (dp, ((y + ROWS - 1) % ROWS) * COLS + x)
    in_row = [(dp, y * COLS + p) for p in peers]
    in_col = [(dp, ((y + j) % ROWS) * COLS + x) for j in range(1, ROWS)]
    core, z = dp % 2, dp // 2
    other = (dp + 1 - 2 * core, c)
    deep = [((z + j) % 8) * 2 + core for j in range(1, 8)]
    load = pltpu.make_async_copy(part, part_v, load_sem.at[0])
    load.start()
    greet(in_row + in_col + [other] + [(to, c) for to in deep])
    before = {}
    started = []

    def hop(step, n, way):
        first = n if way == 0 else 1 - n
        land, stage, ss, rs, to = (
            (down, down_out, dn_s, dn_r, below), (up, up_out, up_s, up_r, above),
        )[way]
        owner = (y + ROWS - 4 + step) % ROWS if way == 0 else (y + 4 - step) % ROWS
        if step == first:
            src = part.at[owner, n]
        else:
            before[way, n].wait_recv()
            stage[step, n] = (
                land[step - 1, n].astype(jnp.float32) + part_v[owner, n].astype(jnp.float32)
            ).astype(jnp.bfloat16)
            src = stage.at[step, n]
        before[way, n] = send(src, land.at[step, n], ss.at[step, n], rs.at[step, n], to)
        started.append(before[way, n])

    hop(0, 0, 0)
    hop(0, 1, 1)
    hop(1, 1, 0)
    hop(1, 0, 1)
    own_q = pltpu.make_async_copy(dqh.at[x], dq.at[:, cols(x * GW, GW)], own_sem.at[0])
    own_q.start()
    back = [
        send(dqh.at[p], dq.at[:, cols(x * GW, GW)], q_s.at[j], q_r.at[j], in_row[j])
        for j, p in enumerate(peers)
    ]
    by[y] = biasp[...]
    col = [send(by.at[y], by.at[y], y_s.at[j], y_r.at[j], t) for j, t in enumerate(in_col)]
    load.wait()
    hop(1, 0, 0)
    hop(1, 1, 1)
    hop(2, 1, 0)
    hop(2, 0, 1)
    hop(2, 0, 0)
    hop(2, 1, 1)
    for copy in col:
        copy.wait_recv()
    bx[x] = jnp.sum(by[...], axis=0)
    wide = [send(bx.at[x], bx.at[x], x_s.at[j], x_r.at[j], t) for j, t in enumerate(in_row)]
    hop(3, 1, 0)
    hop(3, 0, 1)
    for copy in wide:
        copy.wait()
    swap = send(bx, twin, t_s.at[0], t_r.at[0], other)
    hop(3, 0, 0)
    hop(3, 1, 1)
    swap.wait()
    twin[...] += bx[...]
    across = [
        send(twin.at[(to % 8) // 2], bz.at[z], d_s.at[j], d_r.at[j], (to, c))
        for j, to in enumerate(deep)
    ]
    bz[z] = twin[(dp % 8) // 2]
    last = []
    for n, dst in ((1, dkv_v), (0, dkv_k)):
        before[0, n].wait_recv()
        before[1, n].wait_recv()
        total = (
            part_v[y, n].astype(jnp.float32)
            + down[3, n].astype(jnp.float32)
            + up[3, n].astype(jnp.float32)
        )
        final[n] = total.astype(jnp.bfloat16).reshape(COLS, BLK, D)
        for j, p in enumerate(peers):
            last.append(
                send(final.at[n, j + 1], dst.at[:, cols(x * D, D)], f_s.at[j, n], f_r.at[j, n], in_row[j])
            )
        last_own = pltpu.make_async_copy(
            final.at[n, 0], dst.at[:, cols(x * D, D)], own_sem.at[1 + n]
        )
        last_own.start()
        last.append(last_own)
    for copy in across:
        copy.wait()
    entry = jnp.sum(bz[...], axis=0)
    picked = jnp.where(dp < 8, entry[0:1], entry[1:2])
    swapped = jnp.concatenate([picked[:, 64:], picked[:, :64]], axis=1)
    bias[...] = jnp.where(dp % 2 == 0, picked, swapped)
    for copy in started + col:
        copy.wait_send()
    for copy in back + last:
        copy.wait()
    own_q.wait()


def give_back(part, biasp, dqh):
    bf = jnp.bfloat16
    f32 = jnp.float32
    sem = pltpu.SemaphoreType.DMA
    rows = COLS * BLK
    land = ((4, 2, rows, D), bf)
    scratch = [
        ((ROWS, 2, rows, D), bf), land, land, land, land, ((2, COLS, BLK, D), bf),
        ((ROWS, 8, D), f32), ((COLS, 8, D), f32), ((COLS, 8, D), f32), ((8, 8, D), f32),
    ]
    outs = (((BLK, KV * GW), bf), ((BLK, KV * D), bf), ((BLK, KV * D), bf), ((1, D), f32))
    return pl.pallas_call(
        give_back_kernel,
        out_shape=tuple(jax.ShapeDtypeStruct(*s) for s in outs),
        in_specs=[ANY, VMEM, ANY],
        out_specs=[ANY, ANY, ANY, VMEM],
        scratch_shapes=[pltpu.VMEM(*s) for s in scratch] + [
            sem((1,)), sem((3,)), sem((3,)), sem((3,)),
            sem((4, 2)), sem((4, 2)), sem((4, 2)), sem((4, 2)),
            sem((3, 2)), sem((3, 2)),
            sem((7,)), sem((7,)), sem((3,)), sem((3,)), sem((1,)), sem((1,)), sem((7,)), sem((7,)),
        ],
        compiler_params=pltpu.CompilerParams(
            collective_id=1, has_side_effects=True, vmem_limit_bytes=LIMIT
        ),
        name="give_back",
    )(part, biasp, dqh)


def store_kernel(dq, dk, dv, bias, dq_out, dk_out, dv_out, bias_out, dq_v, dk_v, dv_v, sem):
    moves = []
    for n in range(4):
        rows = pl.ds(n * 32, 32)
        moves.append((dq.at[rows], dq_v.at[rows], dq_out.at[rows]))
    moves.append((dk, dk_v, dk_out))
    moves.append((dv, dv_v, dv_out))
    first = [pltpu.make_async_copy(m[0], m[1], sem.at[0, n]) for n, m in enumerate(moves)]
    second = [pltpu.make_async_copy(m[1], m[2], sem.at[1, n]) for n, m in enumerate(moves)]
    for copy in first:
        copy.start()
    bias_out[...] = bias[0, :64]
    for one, two in zip(first, second):
        one.wait()
        two.start()
    for copy in second:
        copy.wait()


def store(dq, dk, dv, bias):
    shape = lambda a: jax.ShapeDtypeStruct(a.shape, a.dtype)
    return pl.pallas_call(
        store_kernel,
        out_shape=(shape(dq), shape(dk), shape(dv), jax.ShapeDtypeStruct((64,), jnp.float32)),
        in_specs=[ANY, ANY, ANY, VMEM],
        out_specs=[ANY, ANY, ANY, VMEM],
        scratch_shapes=[pltpu.VMEM(a.shape, a.dtype) for a in (dq, dk, dv)]
        + [pltpu.SemaphoreType.DMA((2, 6))],
        compiler_params=pltpu.CompilerParams(vmem_limit_bytes=LIMIT),
        name="store",
    )(dq, dk, dv, bias)


def on_device(queries, keys, values, outputs, d_out, log_sums, block_path, live_len):
    gathered = gather(
        block_path, live_len,
        queries[0], d_out[0], outputs[0], keys[0], values[0], jnp.transpose(log_sums, (1, 0, 2)),
    )
    qh, doh, stat, dqt_near, near, far, bias_near = gathered
    part, dqh, biasp = attend(
        block_path, live_len, qh, doh, stat, dqt_near, far, near, bias_near
    )
    dq, dk, dv, bias = store(*give_back(part, biasp, dqh))
    return dq[None], dk[None], dv[None], bias


def solution(mesh):
    wide = P("dp", "ctx", None)
    return jax.shard_map(
        on_device,
        mesh=mesh,
        in_specs=(wide, wide, wide, wide, wide, P("dp", None, "ctx"), P("dp", None), P("dp", None)),
        out_specs=(wide, wide, wide, P("dp")),
        check_vma=False,
    )
```

```python
import functools

import jax
import jax.numpy as jnp
from jax import lax
from jax.experimental import pallas as pl
from jax.experimental.pallas import tpu as pltpu
from jax.sharding import PartitionSpec as P

KV = 4
GROUP = 5
D = 128
BLK = 128
ROWS = 8
COLS = 4
NB = ROWS * COLS
DP = 16
GW = GROUP * D
SCALE = D**-0.5
LOG2E = 1.4426950408889634
FAR = 1e30
FAR_ROWS = ROWS - 3
LIMIT = 60 << 20
MESH = pl.DeviceIdType.MESH
ANY = pl.BlockSpec(memory_space=pl.ANY)
VMEM = pl.BlockSpec(memory_space=pltpu.VMEM)
SMEM = pl.BlockSpec(memory_space=pltpu.SMEM)
NT = (((1,), (1,)), ((), ()))
TN = (((0,), (0,)), ((), ()))


def dot(a, b, dims=(((1,), (0,)), ((), ()))):
    return lax.dot_general(a, b, dims, preferred_element_type=jnp.float32)


def place():
    c = lax.axis_index("ctx")
    return lax.axis_index("dp"), c // COLS, c % COLS


def cols(start, size):
    return pl.ds(pl.multiple_of(start, 128), size)


def greet(targets):
    barrier = pltpu.get_barrier_semaphore()
    for target in targets:
        pl.semaphore_signal(barrier, inc=1, device_id=target, device_id_type=MESH)
    pl.semaphore_wait(barrier, len(targets))


def send(src, dst, send_sem, recv_sem, target):
    copy = pltpu.make_async_remote_copy(
        src_ref=src,
        dst_ref=dst,
        send_sem=send_sem,
        recv_sem=recv_sem,
        device_id=target,
        device_id_type=MESH,
    )
    copy.start()
    return copy


def unit(i, b, row, x, path, kc, vc, qref, gref, stat, dk_at, dv_at, dqt, span=1):
    heads = lambda a: jnp.concatenate([a[:, n * D : (n + 1) * D] for n in range(GROUP)], axis=0)
    flat = lambda first: jnp.concatenate(
        [stat[i, first + n : first + n + 1, :] for n in range(GROUP)], axis=1
    )
    qs, gs = heads(qref[i]), heads(gref[i])
    base, delta = flat(0), flat(8)
    mine = path[0, b]
    s = dot(kc, qs, NT)
    t = dot(vc, gs, NT)
    behind = lax.broadcasted_iota(jnp.int32, (BLK, GW), 0) - (
        lax.broadcasted_iota(jnp.int32, (BLK, GW), 1) % BLK
    )
    p_low, ds = [], []
    for j in range(COLS * span):
        kb = (row + j // COLS) * COLS + (x + j) % COLS
        theirs = path[0, kb]
        joined = (theirs == 0) | (theirs == mine) | (mine == 0)
        shift = base + jnp.where(joined, 0.0, FAR)
        at = slice(j * BLK, (j + 1) * BLK)
        p = jnp.exp2(s[at] * (SCALE * LOG2E) - shift)
        p = jnp.where(behind <= BLK * (b - kb), p, 0.0)
        p_low.append(p.astype(jnp.bfloat16))
        ds.append((p * (t[at] - delta)).astype(jnp.bfloat16))
    p_low = jnp.concatenate(p_low, axis=0)
    ds = jnp.concatenate(ds, axis=0)
    dk_at[...] += dot(ds, qs).reshape(dk_at.shape)
    dv_at[...] += dot(p_low, gs).reshape(dv_at.shape)
    dqt[i] += dot(kc, ds, TN)


def close_row(row, x, live, dk_at, dv_at, part_at, sums):
    key_row = lax.broadcasted_iota(jnp.int32, (BLK, D), 0)
    ka, va = sums
    for j in range(COLS):
        at = slice(j * BLK, (j + 1) * BLK)
        keep = key_row < live[0, row * COLS + (x + j) % COLS]
        a = jnp.where(keep, dk_at[at, :] * SCALE, 0.0)
        b = jnp.where(keep, dv_at[at, :], 0.0)
        part_at[0, at, :] = a.astype(jnp.bfloat16)
        part_at[1, at, :] = b.astype(jnp.bfloat16)
        ka += jnp.sum(a, axis=0, keepdims=True)
        va += jnp.sum(b, axis=0, keepdims=True)
    return ka, va


def no_sums():
    return jnp.zeros((1, D), jnp.float32), jnp.zeros((1, D), jnp.float32)


def gather_kernel(
    path, live, q, do, o, k, v, lse,
    qh, doh, stat, dqt_out, near_out, far, bias,
    do_v, o_v, lse_v, k_v, own_stat, q_v, g_v, kv_all, stat_v, dk, dv, dqt, near_v,
    own_sem, load_sem, out_sem, kv_s, kv_r, q_s, q_r, st_s, st_r, up_s, up_r, dn_s, dn_r,
):
    dp, y, x = place()
    c = y * COLS + x
    peers = [(x + j) % COLS for j in range(1, COLS)]
    above = (dp, ((y + 1) % ROWS) * COLS + x)
    below = (dp, ((y + ROWS - 1) % ROWS) * COLS + x)
    spot = lambda j: pl.ds(j * BLK, BLK)
    rest = pl.ds(BLK, 3 * BLK)
    loads = [
        pltpu.make_async_copy(k, k_v, load_sem.at[0]),
        pltpu.make_async_copy(do, do_v, load_sem.at[1]),
        pltpu.make_async_copy(o, o_v, load_sem.at[2]),
        pltpu.make_async_copy(lse, lse_v, load_sem.at[3]),
    ]
    for copy in loads:
        copy.start()
    own_q = [
        pltpu.make_async_copy(q.at[:, cols(x * GW, GW)], q_v.at[x], own_sem.at[2]),
        pltpu.make_async_copy(do.at[:, cols(x * GW, GW)], g_v.at[x], own_sem.at[3]),
    ]
    own_v = pltpu.make_async_copy(v.at[:, cols(x * D, D)], kv_all.at[y, 1, spot(0)], own_sem.at[1])
    for copy in own_q + [own_v]:
        copy.start()
    greet([(dp, y * COLS + p) for p in peers] + [above, below])
    kv, big = {}, {}
    for j, p in enumerate(peers):
        kv[j, 1] = send(
            v.at[:, cols(p * D, D)], kv_all.at[y, 1, spot(3 - j)], kv_s.at[j, 1], kv_r.at[j, 1],
            (dp, y * COLS + p),
        )
    loads[0].wait()
    key_row = lax.broadcasted_iota(jnp.int32, (BLK, KV * D), 0)
    k_v[...] = jnp.where(key_row < live[0, c], k_v[...].astype(jnp.float32), 0.0).astype(
        jnp.bfloat16
    )
    for j, p in enumerate(peers):
        kv[j, 0] = send(
            k_v.at[:, cols(p * D, D)], kv_all.at[y, 0, spot(3 - j)], kv_s.at[j, 0], kv_r.at[j, 0],
            (dp, y * COLS + p),
        )
    own_k = pltpu.make_async_copy(k_v.at[:, cols(x * D, D)], kv_all.at[y, 0, spot(0)], own_sem.at[0])
    own_k.start()
    ring = {}

    def piece(block, n, part):
        full = kv_all.at[block]
        if part == 0:
            return full.at[:, spot(0)] if n is None else full.at[n, spot(0)]
        return full.at[part - 1, rest]

    def forward(step, part):
        up_block = (y + ROWS - step) % ROWS
        dn_block = (y + step) % ROWS
        half = None if step < 3 else 0
        if step:
            ring[step - 1, part, 0].wait_recv()
        if step < 3 or part != 2:
            at = piece(up_block, half, part)
            ring[step, part, 0] = send(
                at, at, up_s.at[step, part], up_r.at[step, part], above
            )
        if step:
            ring[step - 1, part, 1].wait_recv()
        if step < 3 or part != 1:
            at = piece(dn_block, None if step < 3 else 1, part)
            ring[step, part, 1] = send(
                at, at, dn_s.at[step, part], dn_r.at[step, part], below
            )

    own_v.wait()
    own_k.wait()
    forward(0, 0)
    for j in range(3):
        kv[j, 1].wait_recv()
    forward(0, 2)
    for j in range(3):
        kv[j, 0].wait_recv()
    forward(0, 1)

    def move(*which):
        for j in which:
            for n, (src, dst) in enumerate(((q, q_v), (do, g_v))):
                big[j, n] = send(
                    src.at[:, cols(peers[j] * GW, GW)], dst.at[x], q_s.at[j, n], q_r.at[j, n],
                    (dp, y * COLS + peers[j]),
                )

    move(0, 2)
    for copy in loads[1:]:
        copy.wait()
    ones = jnp.ones((8, D), jnp.bfloat16)
    own_stat[...] = jnp.zeros_like(own_stat)
    for h in range(KV * GROUP):
        g, i = divmod(h, GROUP)
        prod = do_v[:, h * D : (h + 1) * D].astype(jnp.float32) * o_v[
            :, h * D : (h + 1) * D
        ].astype(jnp.float32)
        hi = prod.astype(jnp.bfloat16)
        mid = (prod - hi.astype(jnp.float32)).astype(jnp.bfloat16)
        total = dot(ones, hi, NT) + dot(ones, mid, NT)
        own_stat[g, 8 + i : 9 + i, :] = total[0:1]
        own_stat[g, i : i + 1, :] = lse_v[h] * LOG2E
    stats = [
        send(own_stat.at[p], stat_v.at[x], st_s.at[j], st_r.at[j], (dp, y * COLS + p))
        for j, p in enumerate(peers)
    ]
    mine = pltpu.make_async_copy(own_stat.at[x], stat_v.at[x], own_sem.at[4])
    mine.start()
    dk[...] = jnp.zeros_like(dk)
    dv[...] = jnp.zeros_like(dv)
    dqt[...] = jnp.zeros_like(dqt)

    def pairs(i, row, slot, valid):
        @pl.when(valid)
        def _():
            unit(
                i % COLS, y * COLS + i % COLS, row, x, path, kv_all[row, 0], kv_all[row, 1],
                q_v, g_v, stat_v, dk.at[slot], dv.at[slot], dqt,
            )

    def own_pair(j):
        pairs(x + j, y, 0, y >= 0)

    def last_pair(j):
        pairs(x + j, jnp.maximum(y - 1, 0), 1, y >= 1)

    def back_pair(j):
        pairs(x + j, jnp.maximum(y - 2, 0), 2, y >= 2)

    def open_pair(j):
        pairs(x + j, 0, 3, y >= 6)

    mine.wait()
    for copy in own_q:
        copy.wait()
    forward(1, 0)
    move(1)
    own_pair(0)
    forward(1, 2)
    forward(1, 1)
    last_pair(0)
    for j in (0, 2):
        stats[j].wait_recv()
        big[j, 0].wait_recv()
        big[j, 1].wait_recv()
    forward(2, 0)
    own_pair(1)
    forward(2, 2)
    own_pair(3)
    forward(2, 1)
    last_pair(1)
    last_pair(3)
    back_pair(0)
    forward(3, 0)
    back_pair(1)
    back_pair(3)
    open_pair(0)
    forward(3, 2)
    open_pair(1)
    open_pair(3)
    forward(3, 1)
    stats[1].wait_recv()
    big[1, 0].wait_recv()
    big[1, 1].wait_recv()
    outs = [
        pltpu.make_async_copy(q_v, qh, out_sem.at[0]),
        pltpu.make_async_copy(g_v, doh, out_sem.at[1]),
        pltpu.make_async_copy(stat_v, stat, out_sem.at[2]),
    ]
    for copy in outs:
        copy.start()
    own_pair(2)
    last_pair(2)
    back_pair(2)
    open_pair(2)
    outs.append(pltpu.make_async_copy(dqt, dqt_out, out_sem.at[5]))
    outs[-1].start()
    sums = no_sums()
    for slot, row in enumerate((y, (y + ROWS - 1) % ROWS, (y + ROWS - 2) % ROWS, 0)):
        sums = close_row(row, x, live, dk.at[slot], dv.at[slot], near_v.at[slot], sums)
    outs.append(pltpu.make_async_copy(near_v, near_out, out_sem.at[6]))
    outs[-1].start()
    bias[...] = jnp.zeros_like(bias)
    bias[0:1, :] = sums[0]
    bias[1:2, :] = sums[1]
    for part, way in ((0, 0), (1, 0), (0, 1), (2, 1)):
        ring[3, part, way].wait_recv()
    ends = [pltpu.make_async_copy(kv_all.at[pl.ds(0, FAR_ROWS)], far, out_sem.at[8])]
    for copy in ends:
        copy.start()
    for copy in list(ring.values()) + list(kv.values()) + list(big.values()) + stats:
        copy.wait_send()
    for copy in outs + ends:
        copy.wait()


def gather(path, live, q, do, o, k, v, lse):
    bf = jnp.bfloat16
    f32 = jnp.float32
    sem = pltpu.SemaphoreType.DMA
    rows = COLS * BLK
    heads = ((COLS, BLK, GW), bf)
    whole = ((ROWS, 2, rows, D), bf)
    far = ((FAR_ROWS, 2, rows, D), bf)
    stat = ((COLS, 16, BLK), f32)
    dqt = ((COLS, BLK, GW), f32)
    near = ((4, 2, rows, D), bf)
    outs = [heads, heads, stat, dqt, near, far, ((8, D), f32)]
    full = ((BLK, KV * GW), bf)
    slots = ((4, rows, D), f32)
    scratch = [
        full, full, ((KV * GROUP, 1, BLK), f32), ((BLK, KV * D), bf), stat,
        heads, heads, whole, stat, slots, slots, dqt, near,
    ]
    return pl.pallas_call(
        gather_kernel,
        out_shape=tuple(jax.ShapeDtypeStruct(*s) for s in outs),
        in_specs=[SMEM, SMEM] + [ANY] * 6,
        out_specs=[ANY] * 6 + [VMEM],
        scratch_shapes=[pltpu.VMEM(*s) for s in scratch] + [
            sem((5,)), sem((4,)), sem((9,)), sem((3, 2)), sem((3, 2)), sem((3, 2)), sem((3, 2)),
            sem((3,)), sem((3,)), sem((4, 3)), sem((4, 3)), sem((4, 3)), sem((4, 3)),
        ],
        compiler_params=pltpu.CompilerParams(
            collective_id=0, has_side_effects=True, vmem_limit_bytes=LIMIT
        ),
        name="gather",
    )(path, live, q, do, o, k, v, lse)


def attend_kernel(
    path, live, qh, doh, stat, dqt_near, far, near, bias_near,
    part, dqh, bias,
    q_v, g_v, stat_v, far_v, part_v, dk, dv, dqt, dqh_v, sem, near_sem, out_sem,
):
    y = lax.axis_index("ctx") // COLS
    x = lax.axis_index("ctx") % COLS
    early = y >= 6
    lower = jnp.where(early, 1, 0)
    upper = jnp.maximum(y - 2, 0)
    some = upper > lower
    placed = (
        (0, y, y >= 0), (1, y - 1, y >= 1), (2, y - 2, y >= 2), (3, 0, early),
    )
    near_copy = lambda slot, row: pltpu.make_async_copy(
        near.at[slot], part_v.at[row], near_sem.at[slot]
    )
    loads = [
        pltpu.make_async_copy(src, dst, sem.at[n])
        for n, (src, dst) in enumerate(
            ((far, far_v), (qh, q_v), (stat, stat_v), (doh, g_v))
        )
    ]

    @pl.when(some)
    def _():
        for copy in loads:
            copy.start()

    for slot, row, valid in placed:

        @pl.when(valid)
        def _(slot=slot, row=row):
            near_copy(slot, row).start()

    def blank(n, _):
        part_v[n] = jnp.zeros((2, COLS * BLK, D), jnp.bfloat16)
        return 0

    lax.fori_loop(y + 1, ROWS, blank, 0)
    out_q = pltpu.make_async_copy(dqh_v, dqh, out_sem.at[0])
    load_q = pltpu.make_async_copy(dqt_near, dqt, sem.at[4])
    load_q.start()

    def clear(n, _):
        dk[n] = jnp.zeros((COLS * BLK, D), jnp.float32)
        dv[n] = jnp.zeros((COLS * BLK, D), jnp.float32)
        return 0

    lax.fori_loop(lower, upper, clear, 0)
    load_q.wait()

    @pl.when(some)
    def _():
        for copy in loads:
            copy.wait()

        def query(i, _):
            b = y * COLS + i
            mine = path[0, b]

            def one(row, _):
                seen = lambda kb: (path[0, kb] == 0) | (path[0, kb] == mine) | (mine == 0)
                kb = row * COLS
                needed = seen(kb) | seen(kb + 1) | seen(kb + 2) | seen(kb + 3)

                @pl.when(needed)
                def _():
                    unit(
                        i, b, row, x, path, far_v[row, 0], far_v[row, 1], q_v, g_v, stat_v,
                        dk.at[row], dv.at[row], dqt,
                    )

                return 0

            def two(n, _):
                at = pl.ds(lower + 2 * n, 2)
                wide = (2 * COLS * BLK, D)
                unit(
                    i, b, lower + 2 * n, x, path,
                    far_v[at, 0].reshape(wide), far_v[at, 1].reshape(wide),
                    q_v, g_v, stat_v, dk.at[at], dv.at[at], dqt, 2,
                )
                return 0

            twos = jnp.where(mine == 0, (upper - lower) // 2, 0)
            lax.fori_loop(0, twos, two, 0)
            lax.fori_loop(lower + 2 * twos, upper, one, 0)
            return 0

        lax.fori_loop(0, COLS, query, 0)

    def finish_query(i, _):
        for n in range(GROUP):
            at = slice(n * D, (n + 1) * D)
            dqh_v[i, :, at] = (dqt[i, :, at] * SCALE).T.astype(jnp.bfloat16)
        return 0

    lax.fori_loop(0, COLS, finish_query, 0)
    out_q.start()

    sums = lax.fori_loop(
        lower,
        upper,
        lambda n, s: close_row(n, x, live, dk.at[n], dv.at[n], part_v.at[n], s),
        (bias_near[0:1, :], bias_near[1:2, :]),
    )
    bias[...] = jnp.zeros_like(bias)
    bias[0:1, :] = sums[0]
    bias[1:2, :] = sums[1]
    for slot, row, valid in placed:

        @pl.when(valid)
        def _(slot=slot, row=row):
            near_copy(slot, row).wait()

    out_part = pltpu.make_async_copy(part_v, part, out_sem.at[1])
    out_part.start()
    out_part.wait()
    out_q.wait()


def attend(path, live, qh, doh, stat, dqt_near, far, near, bias_near):
    bf = jnp.bfloat16
    f32 = jnp.float32
    rows = COLS * BLK
    sem = pltpu.SemaphoreType.DMA
    heads = ((COLS, BLK, GW), bf)
    kept = ((FAR_ROWS, 2, rows, D), bf)
    part = ((ROWS, 2, rows, D), bf)
    dqt = ((COLS, BLK, GW), f32)
    grads = ((FAR_ROWS, rows, D), f32)
    scratch = [heads, heads, ((COLS, 16, BLK), f32), kept, part, grads, grads, dqt, heads]
    return pl.pallas_call(
        attend_kernel,
        out_shape=tuple(jax.ShapeDtypeStruct(*s) for s in (part, heads, ((8, D), f32))),
        in_specs=[SMEM, SMEM] + [ANY] * 6 + [VMEM],
        out_specs=[ANY, ANY, VMEM],
        scratch_shapes=[pltpu.VMEM(*s) for s in scratch] + [sem((5,)), sem((4,)), sem((2,))],
        compiler_params=pltpu.CompilerParams(vmem_limit_bytes=LIMIT),
        name="attend",
    )(path, live, qh, doh, stat, dqt_near, far, near, bias_near)


def give_back_kernel(
    part, biasp, dqh,
    dq, dkv_k, dkv_v, bias,
    part_v, down, up, down_out, up_out, final, by, bx, twin, bz,
    load_sem, own_sem, q_s, q_r, dn_s, dn_r, up_s, up_r, f_s, f_r, y_s, y_r, x_s, x_r, t_s, t_r, d_s, d_r,
):
    dp, y, x = place()
    c = y * COLS + x
    peers = [(x + j) % COLS for j in range(1, COLS)]
    above = (dp, ((y + 1) % ROWS) * COLS + x)
    below = (dp, ((y + ROWS - 1) % ROWS) * COLS + x)
    in_row = [(dp, y * COLS + p) for p in peers]
    in_col = [(dp, ((y + j) % ROWS) * COLS + x) for j in range(1, ROWS)]
    core, z = dp % 2, dp // 2
    other = (dp + 1 - 2 * core, c)
    deep = [((z + j) % 8) * 2 + core for j in range(1, 8)]
    load = pltpu.make_async_copy(part, part_v, load_sem.at[0])
    load.start()
    greet(in_row + in_col + [other] + [(to, c) for to in deep])
    before = {}
    started = []

    def hop(step, n, way):
        first = n if way == 0 else 1 - n
        land, stage, ss, rs, to = (
            (down, down_out, dn_s, dn_r, below), (up, up_out, up_s, up_r, above),
        )[way]
        owner = (y + ROWS - 4 + step) % ROWS if way == 0 else (y + 4 - step) % ROWS
        if step == first:
            src = part.at[owner, n]
        else:
            before[way, n].wait_recv()
            stage[step, n] = (
                land[step - 1, n].astype(jnp.float32) + part_v[owner, n].astype(jnp.float32)
            ).astype(jnp.bfloat16)
            src = stage.at[step, n]
        before[way, n] = send(src, land.at[step, n], ss.at[step, n], rs.at[step, n], to)
        started.append(before[way, n])

    hop(0, 0, 0)
    hop(0, 1, 1)
    hop(1, 1, 0)
    hop(1, 0, 1)
    own_q = pltpu.make_async_copy(dqh.at[x], dq.at[:, cols(x * GW, GW)], own_sem.at[0])
    own_q.start()
    back = [
        send(dqh.at[p], dq.at[:, cols(x * GW, GW)], q_s.at[j], q_r.at[j], in_row[j])
        for j, p in enumerate(peers)
    ]
    by[y] = biasp[...]
    col = [send(by.at[y], by.at[y], y_s.at[j], y_r.at[j], t) for j, t in enumerate(in_col)]
    load.wait()
    hop(1, 0, 0)
    hop(1, 1, 1)
    hop(2, 1, 0)
    hop(2, 0, 1)
    hop(2, 0, 0)
    hop(2, 1, 1)
    for copy in col:
        copy.wait_recv()
    bx[x] = jnp.sum(by[...], axis=0)
    wide = [send(bx.at[x], bx.at[x], x_s.at[j], x_r.at[j], t) for j, t in enumerate(in_row)]
    hop(3, 1, 0)
    hop(3, 0, 1)
    for copy in wide:
        copy.wait()
    swap = send(bx, twin, t_s.at[0], t_r.at[0], other)
    hop(3, 0, 0)
    hop(3, 1, 1)
    swap.wait()
    twin[...] += bx[...]
    across = [
        send(twin.at[(to % 8) // 2], bz.at[z], d_s.at[j], d_r.at[j], (to, c))
        for j, to in enumerate(deep)
    ]
    bz[z] = twin[(dp % 8) // 2]
    last = []
    for n, dst in ((1, dkv_v), (0, dkv_k)):
        before[0, n].wait_recv()
        before[1, n].wait_recv()
        total = (
            part_v[y, n].astype(jnp.float32)
            + down[3, n].astype(jnp.float32)
            + up[3, n].astype(jnp.float32)
        )
        final[n] = total.astype(jnp.bfloat16).reshape(COLS, BLK, D)
        for j, p in enumerate(peers):
            last.append(
                send(final.at[n, j + 1], dst.at[:, cols(x * D, D)], f_s.at[j, n], f_r.at[j, n], in_row[j])
            )
        last_own = pltpu.make_async_copy(
            final.at[n, 0], dst.at[:, cols(x * D, D)], own_sem.at[1 + n]
        )
        last_own.start()
        last.append(last_own)
    for copy in across:
        copy.wait()
    entry = jnp.sum(bz[...], axis=0)
    picked = jnp.where(dp < 8, entry[0:1], entry[1:2])
    swapped = jnp.concatenate([picked[:, 64:], picked[:, :64]], axis=1)
    bias[...] = jnp.where(dp % 2 == 0, picked, swapped)
    for copy in started + col:
        copy.wait_send()
    for copy in back + last:
        copy.wait()
    own_q.wait()


def give_back(part, biasp, dqh):
    bf = jnp.bfloat16
    f32 = jnp.float32
    sem = pltpu.SemaphoreType.DMA
    rows = COLS * BLK
    land = ((4, 2, rows, D), bf)
    scratch = [
        ((ROWS, 2, rows, D), bf), land, land, land, land, ((2, COLS, BLK, D), bf),
        ((ROWS, 8, D), f32), ((COLS, 8, D), f32), ((COLS, 8, D), f32), ((8, 8, D), f32),
    ]
    outs = (((BLK, KV * GW), bf), ((BLK, KV * D), bf), ((BLK, KV * D), bf), ((1, D), f32))
    return pl.pallas_call(
        give_back_kernel,
        out_shape=tuple(jax.ShapeDtypeStruct(*s) for s in outs),
        in_specs=[ANY, VMEM, ANY],
        out_specs=[ANY, ANY, ANY, VMEM],
        scratch_shapes=[pltpu.VMEM(*s) for s in scratch] + [
            sem((1,)), sem((3,)), sem((3,)), sem((3,)),
            sem((4, 2)), sem((4, 2)), sem((4, 2)), sem((4, 2)),
            sem((3, 2)), sem((3, 2)),
            sem((7,)), sem((7,)), sem((3,)), sem((3,)), sem((1,)), sem((1,)), sem((7,)), sem((7,)),
        ],
        compiler_params=pltpu.CompilerParams(
            collective_id=1, has_side_effects=True, vmem_limit_bytes=LIMIT
        ),
        name="give_back",
    )(part, biasp, dqh)


def store_kernel(dq, dk, dv, bias, dq_out, dk_out, dv_out, bias_out, dq_v, dk_v, dv_v, sem):
    moves = []
    for n in range(4):
        rows = pl.ds(n * 32, 32)
        moves.append((dq.at[rows], dq_v.at[rows], dq_out.at[rows]))
    moves.append((dk, dk_v, dk_out))
    moves.append((dv, dv_v, dv_out))
    first = [pltpu.make_async_copy(m[0], m[1], sem.at[0, n]) for n, m in enumerate(moves)]
    second = [pltpu.make_async_copy(m[1], m[2], sem.at[1, n]) for n, m in enumerate(moves)]
    for copy in first:
        copy.start()
    bias_out[...] = bias[0, :64]
    for one, two in zip(first, second):
        one.wait()
        two.start()
    for copy in second:
        copy.wait()


def store(dq, dk, dv, bias):
    shape = lambda a: jax.ShapeDtypeStruct(a.shape, a.dtype)
    return pl.pallas_call(
        store_kernel,
        out_shape=(shape(dq), shape(dk), shape(dv), jax.ShapeDtypeStruct((64,), jnp.float32)),
        in_specs=[ANY, ANY, ANY, VMEM],
        out_specs=[ANY, ANY, ANY, VMEM],
        scratch_shapes=[pltpu.VMEM(a.shape, a.dtype) for a in (dq, dk, dv)]
        + [pltpu.SemaphoreType.DMA((2, 6))],
        compiler_params=pltpu.CompilerParams(vmem_limit_bytes=LIMIT),
        name="store",
    )(dq, dk, dv, bias)


def on_device(queries, keys, values, outputs, d_out, log_sums, block_path, live_len):
    gathered = gather(
        block_path, live_len,
        queries[0], d_out[0], outputs[0], keys[0], values[0], jnp.transpose(log_sums, (1, 0, 2)),
    )
    qh, doh, stat, dqt_near, near, far, bias_near = gathered
    part, dqh, biasp = attend(
        block_path, live_len, qh, doh, stat, dqt_near, far, near, bias_near
    )
    dq, dk, dv, bias = store(*give_back(part, biasp, dqh))
    return dq[None], dk[None], dv[None], bias


def solution(mesh):
    wide = P("dp", "ctx", None)
    return jax.shard_map(
        on_device,
        mesh=mesh,
        in_specs=(wide, wide, wide, wide, wide, P("dp", None, "ctx"), P("dp", None), P("dp", None)),
        out_specs=(wide, wide, wide, P("dp")),
        check_vma=False,
    )
```
